32 devices in a mesh: tx: 4 (over y, x), ty: 2 (over core), ea: 4 (over z).
Axes of the slice: x: 2, y: 2, z: 4, core: 2. Of those that a mesh axis runs over, the one named last changes fastest.
Arguments:
- science: float32 [4, 512, 512], P('ea', 'tx', 'ty'), may hold values from -6 to 6
- inv_variance: float32 [4, 512, 512], P('ea', 'tx', 'ty'), may hold values from 0.25 to 4
- psf_taps: float32 [4, 9], P('ea'), may hold values from 0.05 to 1
- epoch_times: int32 [4], replicated, may hold values from 0 to 256, as said below
- velocities: int32 [24, 2], P('ea'), may hold values from -15 to 15
Outputs:
- likelihood: float32 [24, 512, 512], P('ea', 'tx', 'ty')
The draws below stay inside these ranges and needn't reach their ends.
Inputs may be any that keep to these rules, and one draw needn't show every extreme that they name: `epoch_times`: the first epoch has time 0 and the last has time 256.
All inputs are finite; a program needn't handle non-finite values.
Results may differ from the reference program's by a relative error of at most 0.0053.
Values may be sent and summed in bfloat16 or wider, within the bound.
No kernel may reach another device: no remote copies, remote signals or barrier semaphores. Data moves between devices by JAX's collectives and lax.ppermute only.
A program may use at most 64 MiB of HBM per device.

```python
import math
import jax
import jax.numpy as jnp
from jax import lax

REACH = 32
PR = 4
VMAX = 15
EPOCHS = 4
HYPS = 24
NROWS = 512
NCOLS = 512
TSPAN = 256
TAPS = 9


def draw_epoch_times(key, part):
    values = jax.random.randint(key, (EPOCHS,), 0, TSPAN + 1).astype(jnp.int32)
    values = values.at[0].set(0)
    values = values.at[EPOCHS - 1].set(TSPAN)
    return values


def plant(result, own_key, low, top_value):
    longest = result.shape.index(max(result.shape))
    spots = []
    for shift in (0, 1):
        where = [jax.random.randint(jax.random.fold_in(own_key, axis), (), 0, length) for axis, length in enumerate(result.shape)]
        where[longest] = (where[longest] + shift) % result.shape[longest]
        spots.append(tuple(where))
    return result.at[spots[0]].set(low).at[spots[1]].set(top_value)


def block_scale(key, shape, shards, low, largest):
    factor_of = 1.0
    for axis_at, parts in shards:
        draws = jax.random.uniform(jax.random.fold_in(jax.random.fold_in(key, 6), axis_at), (parts,), jnp.float32, low / len(shards), largest / len(shards))
        factor_of = factor_of * jnp.repeat(jnp.exp(draws), shape[axis_at] // parts).reshape((-1,) + (1,) * (len(shape) - 1 - axis_at))
    return factor_of


def normal_values(rng, extent, spread, most, shards=(), kind=jnp.bfloat16):
    result = spread * jax.random.normal(rng, extent, jnp.float32)
    if shards:
        result = result * block_scale(rng, extent, shards, -0.22, 0.18)
    return jnp.clip(result, -most, most).astype(kind)


def setup_inputs(seed: int = 0) -> dict:
    seeds = jax.random.split(jax.random.key(seed), 6)
    return {
        "science": normal_values(seeds[0], (EPOCHS, NROWS, NCOLS), 1.0, 6.0, ((0, 4), (1, 4), (2, 2)), jnp.float32),
        "inv_variance": jnp.clip(jnp.exp(math.log(4.0) - 2.7725887 * jax.random.uniform(seeds[1], (EPOCHS, NROWS, NCOLS), jnp.float32) ** block_scale(seeds[1], (EPOCHS, NROWS, NCOLS), ((0, 4), (1, 4), (2, 2)), -0.2, 0.2)), 0.25, 4.0),
        "psf_taps": jnp.clip(jnp.exp(math.log(1.0) - 2.9957323 * jax.random.uniform(seeds[2], (EPOCHS, TAPS), jnp.float32) ** block_scale(seeds[2], (EPOCHS, TAPS), ((0, 4),), -0.2, 0.2)), 0.05, 1.0),
        "epoch_times": draw_epoch_times(jax.random.fold_in(seeds[5], 71), 0),
        "velocities": plant(jax.random.randint(seeds[4], (HYPS, 2), 0 - VMAX, VMAX + 1), jax.random.fold_in(seeds[4], 1), 0 - VMAX, VMAX).astype(jnp.int32),
    }


def blur(field, kern):
    count = kern.shape[1]
    rows = field.shape[1] - count + 1
    acc = kern[:, 0, None, None] * field[:, 0:rows, :]
    for k in range(1, count):
        acc = acc + kern[:, k, None, None] * field[:, k:k + rows, :]
    cols = acc.shape[2] - count + 1
    out = kern[:, 0, None, None] * acc[:, :, 0:cols]
    for k in range(1, count):
        out = out + kern[:, k, None, None] * acc[:, :, k:k + cols]
    return out

def spline_taps(speed, tvals):
    moved = jnp.floor_divide(speed * tvals, 8)
    whole = jnp.floor_divide(moved, 16)
    frac = (moved - 16 * whole).astype(jnp.float32) / 16.0
    frac2 = frac * frac
    frac3 = frac2 * frac
    weights = jnp.stack([(1.0 - frac) ** 3 / 6.0, (3.0 * frac3 - 6.0 * frac2 + 4.0) / 6.0, (-3.0 * frac3 + 3.0 * frac2 + 3.0 * frac + 1.0) / 6.0, frac3 / 6.0], -1)
    return (whole.astype(jnp.int32), weights.astype(jnp.bfloat16))

def reference(science, inv_variance, psf_taps, epoch_times, velocities):
    kern_p = psf_taps / lax.optimization_barrier(jnp.sum(psf_taps, axis=1, keepdims=True))
    kern_q = kern_p * kern_p
    weighted = science * inv_variance
    pad_psf = ((0, 0), (PR, PR), (PR, PR))
    psi = blur(jnp.pad(weighted, pad_psf), kern_p).astype(jnp.bfloat16)
    phi = blur(jnp.pad(inv_variance, pad_psf), kern_q).astype(jnp.bfloat16)
    images = jnp.stack([psi, phi], 1)
    padded = jnp.pad(images, ((0, 0), (0, 0), (REACH, REACH), (REACH, REACH)))

    def one_epoch(image, whole_r, w_r, whole_c, w_c):
        rows_acc = jnp.zeros((2, NROWS, padded.shape[3]), jnp.float32)
        for a in range(4):
            start = (REACH + whole_r + a - 1).astype(jnp.int32)
            piece = lax.dynamic_slice_in_dim(image, start, NROWS, axis=1).astype(jnp.float32)
            rows_acc = rows_acc + w_r[a].astype(jnp.float32) * piece
        moved_rows = rows_acc.astype(jnp.bfloat16)
        out = jnp.zeros((2, NROWS, NCOLS), jnp.float32)
        for b in range(4):
            start = (REACH + whole_c + b - 1).astype(jnp.int32)
            piece = lax.dynamic_slice_in_dim(moved_rows, start, NCOLS, axis=2).astype(jnp.float32)
            out = out + w_c[b].astype(jnp.float32) * piece
        return out

    def one_hyp(speed):
        whole_r, w_r = spline_taps(speed[0], epoch_times)
        whole_c, w_c = spline_taps(speed[1], epoch_times)
        terms = jax.vmap(one_epoch)(padded, whole_r, w_r, whole_c, w_c)
        sums = lax.optimization_barrier(jnp.sum(terms, axis=0))
        return sums[0] / jnp.sqrt(sums[1])
    return lax.map(one_hyp, velocities)
```

```python
import functools

import jax
import jax.numpy as jnp
from jax import lax
from jax.experimental import pallas as pl
from jax.experimental.pallas import tpu as pltpu
from jax.sharding import PartitionSpec as P

REACH = 32
PR = 4
RIM = 40
HALF = 64
GROUP = 4
VMEM_LIMIT = 60 * 1024 * 1024


def spline_taps(speed, tvals):
    moved = jnp.floor_divide(speed * tvals, 8)
    whole = jnp.floor_divide(moved, 16)
    frac = (moved - 16 * whole).astype(jnp.float32) / 16.0
    frac2 = frac * frac
    frac3 = frac2 * frac
    weights = jnp.stack(
        [
            (1.0 - frac) ** 3 / 6.0,
            (3.0 * frac3 - 6.0 * frac2 + 4.0) / 6.0,
            (-3.0 * frac3 + 3.0 * frac2 + 3.0 * frac + 1.0) / 6.0,
            frac3 / 6.0,
        ],
        -1,
    )
    return (whole, weights.astype(jnp.bfloat16))


def pack_kernel(sci_ref, iv_ref, taps_ref, out_ref):
    rows, cols = sci_ref.shape[1:]
    iv = iv_ref[0]
    out_ref[0:rows, :] = (sci_ref[0] * iv).astype(jnp.bfloat16)
    out_ref[rows : 2 * rows, :] = iv.astype(jnp.bfloat16)
    taps = taps_ref[...]
    p = taps / jnp.sum(taps, axis=1, keepdims=True)
    p = jnp.concatenate([p, jnp.zeros((1, cols - p.shape[1]), jnp.float32)], axis=1)
    hi = p.astype(jnp.bfloat16).astype(jnp.float32)
    mid = (p - hi).astype(jnp.bfloat16).astype(jnp.float32)
    low = p - hi - mid
    row = lax.broadcasted_iota(jnp.int32, (16, cols), 0)
    block = jnp.where(row == 0, hi, jnp.where(row == 1, mid, jnp.where(row == 2, low, 0.0)))
    out_ref[2 * rows :, :] = block.astype(jnp.bfloat16)


def strip_kernel(rows, *refs):
    count = len(refs) - 2
    up_ref, down_ref = refs[count:]
    for k in range(count):
        both = [refs[k][i * rows : (i + 1) * rows, :].astype(jnp.float32) for i in range(2)]
        up_ref[k] = jnp.concatenate([x[:RIM] for x in both], 0).astype(jnp.bfloat16)
        down_ref[k] = jnp.concatenate([x[rows - RIM :] for x in both], 0).astype(jnp.bfloat16)


def band(shape, count, first, weights, row_axis):
    source = lax.broadcasted_iota(jnp.int32, shape, 1 - row_axis)
    target = lax.broadcasted_iota(jnp.int32, shape, row_axis)
    d = source - target - first
    d = jnp.where(d >= count, d - count, d)
    acc = jnp.zeros(shape, jnp.float32)
    for a, w in enumerate(weights):
        acc = jnp.where(d == a, w, acc)
    return acc.astype(jnp.bfloat16)


def shift_kernel(hyps, rows, rim_rows, rim_cols, whole_ref, w_ref, rb_ref, cb_ref):
    def one(index, carry):
        e = index // hyps
        h = index % hyps
        at = index * 2
        ws = [w_ref[at * 4 + a] for a in range(4)]
        rb_ref[e, pl.ds(pl.multiple_of(h * rows, rows), rows), :] = band(
            (rows, rim_rows), rim_rows, whole_ref[at] - 1, ws, 0
        )
        ws = [w_ref[at * 4 + 4 + a] for a in range(4)]
        cb_ref[h, e] = band((rim_cols, 128), rim_cols, whole_ref[at + 1] - 1, ws, 1)
        return carry

    lax.fori_loop(0, rb_ref.shape[0] * hyps, one, 0)


def circle(position, count, last):
    return jnp.where(position < last, position, position - count)


def blur_kernel(rows, cols, place_ref, *refs):
    count = len(refs) - 2
    br_ref, bc_ref = refs[count:]
    out_rows, in_rows = br_ref.shape[2:]
    all_cols = bc_ref.shape[2]
    low_row = place_ref[0]
    high_row = place_ref[1]
    low_col = place_ref[2]
    high_col = place_ref[3]
    n = circle(lax.broadcasted_iota(jnp.int32, (out_rows, in_rows), 0), out_rows, rows + REACH)
    k = circle(lax.broadcasted_iota(jnp.int32, (out_rows, in_rows), 1), in_rows, rows + HALF)
    d_r = jnp.where((n >= low_row) & (n < high_row), k - n + PR, -1)
    k = circle(lax.broadcasted_iota(jnp.int32, (all_cols, all_cols), 0), all_cols, cols + HALF)
    n = circle(lax.broadcasted_iota(jnp.int32, (all_cols, all_cols), 1), all_cols, cols + HALF)
    d_c = jnp.where((n >= low_col) & (n < high_col), k - n + PR, -1)
    for e in range(count):
        block = refs[e][2 * rows : 2 * rows + 16, :].astype(jnp.float32)
        p = block[0:1] + block[1:2] + block[2:3]
        q = p * p
        for d, ref in ((d_r, br_ref), (d_c, bc_ref)):
            acc_p = jnp.zeros(d.shape, jnp.float32)
            acc_q = acc_p
            for t in range(2 * PR + 1):
                hit = d == t
                acc_p = jnp.where(hit, p[:, t : t + 1], acc_p)
                acc_q = jnp.where(hit, q[:, t : t + 1], acc_q)
            ref[e, 0] = acc_p.astype(jnp.bfloat16)
            ref[e, 1] = acc_q.astype(jnp.bfloat16)


def dot(a, b):
    return jnp.dot(a, b, preferred_element_type=jnp.float32)


def stack_kernel(slots, hyps, rows, cols, first, final, side_ref, *refs):
    refs = list(refs)
    tiles = [refs.pop(0) for _ in range(slots)]
    above, below, side_tile, side_above, side_below, br, bc, rb, cb = [refs.pop(0) for _ in range(9)]
    acc_in = None if first else refs.pop(0)
    out, moved = refs
    rim_rows = br.shape[2]
    in_rows = br.shape[3]
    lane = lax.broadcasted_iota(jnp.int32, (1, 128), 1)
    keep = jnp.where(lane < HALF, side_ref[0], side_ref[1]) > 0
    for e in range(slots):
        pair = []
        for i in range(2):
            at = slice(i * rows, (i + 1) * rows)
            rim = slice(i * RIM, (i + 1) * RIM)
            left = jnp.concatenate(
                [
                    tiles[e][at, :].astype(jnp.float32),
                    below[e].astype(jnp.float32)[rim],
                    jnp.zeros((in_rows - rows - 2 * RIM, cols), jnp.float32),
                    above[e].astype(jnp.float32)[rim],
                ],
                0,
            )
            right = jnp.concatenate(
                [
                    side_tile[e, at, :].astype(jnp.float32),
                    side_below[e].astype(jnp.float32)[rim],
                    jnp.zeros((in_rows - rows - 2 * RIM, 128), jnp.float32),
                    side_above[e].astype(jnp.float32)[rim],
                ],
                0,
            )
            field = jnp.concatenate([left, jnp.where(keep, right, 0.0)], 1).astype(jnp.bfloat16)
            half = dot(br[e, i], field).astype(jnp.bfloat16)
            pair.append(dot(half, bc[e, i]).astype(jnp.bfloat16))
        both = jnp.concatenate(pair, 1)
        wide = pair[0].shape[1]
        for h in range(hyps):
            m = dot(rb[e, h * rows : (h + 1) * rows, :], both).astype(jnp.bfloat16)
            moved[h, 0:rows, e * wide : (e + 1) * wide] = m[:, :wide]
            moved[h, rows : 2 * rows, e * wide : (e + 1) * wide] = m[:, wide:]
    for h in range(hyps):
        cols_band = []
        for e in range(slots):
            c = cb[h, e]
            ends = c.shape[0] - 128
            cols_band.append(
                jnp.concatenate([c, jnp.concatenate([c[ends:], c[:ends]], 0)], 1)
            )
        total = dot(moved[h], jnp.concatenate(cols_band, 0))
        if acc_in is not None:
            total = total + acc_in[h]
        if final:
            out[h] = total[:rows] / jnp.sqrt(total[rows:])
        else:
            out[h] = total


VMEM = pl.BlockSpec(memory_space=pltpu.VMEM)
SMEM = pl.BlockSpec(memory_space=pltpu.SMEM)
PARAMS = pltpu.CompilerParams(vmem_limit_bytes=VMEM_LIMIT)


def call(kernel, specs, shapes, *args, scratch=(), flops=0, bytes_accessed=0):
    single = not isinstance(shapes, (list, tuple))
    return pl.pallas_call(
        kernel,
        out_shape=shapes,
        in_specs=specs,
        out_specs=VMEM if single else [VMEM] * len(shapes),
        scratch_shapes=list(scratch),
        compiler_params=PARAMS,
        cost_estimate=pl.CostEstimate(
            flops=flops, bytes_accessed=bytes_accessed, transcendentals=0
        ),
    )(*args)


def bf16(*shape):
    return jax.ShapeDtypeStruct(shape, jnp.bfloat16)


def side_swap(x):
    count = lax.axis_size("ty")
    me = lax.axis_index("ty")
    head = x[..., :128]
    tail = x[..., x.shape[-1] - 128 :]
    if count == 2:
        return lax.ppermute(jnp.where(me == 0, tail, head), "ty", [(0, 1), (1, 0)])
    after = lax.ppermute(head, "ty", [(i + 1, i) for i in range(count - 1)])
    before = lax.ppermute(tail, "ty", [(i, i + 1) for i in range(count - 1)])
    lane = lax.broadcasted_iota(jnp.int32, x.shape[:-1] + (128,), x.ndim - 1)
    return jnp.where(lane < HALF, after, before)


def shards(science, inv_variance, psf_taps, epoch_times, velocities):
    rows, cols = science.shape[1:]
    hyps = velocities.shape[0]
    epochs = lax.axis_size("ea")
    tx = lax.axis_size("tx")
    ty = lax.axis_size("ty")
    here_x = lax.axis_index("tx")
    here_y = lax.axis_index("ty")
    here_e = lax.axis_index("ea")
    rim_rows = rows + 2 * REACH
    in_rows = rows + 2 * HALF
    all_cols = cols + 2 * HALF
    slots = min(GROUP, epochs)

    own = call(pack_kernel, [VMEM] * 3, bf16(2 * rows + 16, cols), science, inv_variance, psf_taps)
    payload = [own] + [
        lax.ppermute(own, "ea", [(i, i ^ k) for i in range(epochs)]) for k in range(1, epochs)
    ]

    order = here_e ^ jnp.arange(epochs, dtype=jnp.int32)
    times = epoch_times[order]
    whole, weights = spline_taps(velocities[None, :, :], times[:, None, None])
    weights = weights.astype(jnp.float32)

    low_row = jnp.where(here_x == 0, 0, -REACH)
    high_row = jnp.where(here_x == tx - 1, rows, rows + REACH)
    low_col = jnp.where(here_y == 0, 0, -REACH)
    high_col = jnp.where(here_y == ty - 1, cols, cols + REACH)
    place = jnp.stack([low_row, high_row, low_col, high_col]).astype(jnp.int32)
    side = jnp.stack([here_y < ty - 1, here_y > 0]).astype(jnp.int32)

    def group(tiles, whole, weights, total, final):
        up, down = call(
            functools.partial(strip_kernel, rows),
            [VMEM] * slots,
            [bf16(slots, 2 * RIM, cols)] * 2,
            *tiles,
        )
        above = lax.ppermute(down, "tx", [(i, i + 1) for i in range(tx - 1)])
        below = lax.ppermute(up, "tx", [(i + 1, i) for i in range(tx - 1)])
        side_tile = side_swap(jnp.stack(tiles))
        side_above = side_swap(above)
        side_below = side_swap(below)
        rb, cb = call(
            functools.partial(shift_kernel, hyps, rows, rim_rows, all_cols),
            [SMEM] * 2,
            [bf16(slots, hyps * rows, rim_rows), bf16(hyps, slots, all_cols, 128)],
            whole.reshape(-1),
            weights.reshape(-1),
        )
        br, bc = call(
            functools.partial(blur_kernel, rows, cols),
            [SMEM] + [VMEM] * slots,
            [bf16(slots, 2, rim_rows, in_rows), bf16(slots, 2, all_cols, all_cols)],
            place,
            *tiles,
        )
        args = [side, *tiles, above, below, side_tile, side_above, side_below, br, bc, rb, cb]
        if total is not None:
            args.append(total)
        shape = (hyps, rows, cols) if final else (hyps, 2 * rows, cols)
        return call(
            functools.partial(stack_kernel, slots, hyps, rows, cols, total is None, final),
            [SMEM] + [VMEM] * (len(args) - 1),
            jax.ShapeDtypeStruct(shape, jnp.float32),
            *args,
            scratch=[pltpu.VMEM((hyps, 2 * rows, slots * all_cols), jnp.bfloat16)],
        )

    if epochs == slots:
        return group(payload, whole, weights, None, True)

    def step(total, xs):
        tiles, whole, weights = xs
        return group([tiles[k] for k in range(slots)], whole, weights, total, False), None

    split = lambda x: x.reshape((epochs // slots, slots) + x.shape[1:])
    zeros = jnp.zeros((hyps, 2 * rows, cols), jnp.float32)
    total, _ = lax.scan(step, zeros, (split(jnp.stack(payload)), split(whole), split(weights)))
    return total[:, :rows] / jnp.sqrt(total[:, rows:])


def solution(mesh):
    in_specs = (P("ea", "tx", "ty"), P("ea", "tx", "ty"), P("ea", None), P(), P("ea", None))
    out_specs = P("ea", "tx", "ty")
    return jax.shard_map(shards, mesh=mesh, in_specs=in_specs, out_specs=out_specs, check_vma=False)
```

```python
import functools

import jax
import jax.numpy as jnp
from jax import lax
from jax.experimental import pallas as pl
from jax.experimental.pallas import tpu as pltpu
from jax.sharding import PartitionSpec as P

REACH = 32
PR = 4
RIM = REACH + PR
GROUP = 4
VMEM_LIMIT = 24 * 1024 * 1024
STRIP_FLOPS = 10_000_000
SHIFT_FLOPS = 4_000_000_000
BLUR_FLOPS = 4_000_000_000
STACK_FLOPS = 2_000_000_000


def spline_taps(speed, time):
    moved = (speed * time) >> 3
    frac = (moved & 15).astype(jnp.float32) * (1.0 / 16.0)
    rest = 1.0 - frac
    frac2 = frac * frac
    frac3 = frac2 * frac
    sixth = 1.0 / 6.0
    weights = [
        rest * rest * rest * sixth,
        (3.0 * frac3 - 6.0 * frac2 + 4.0) * sixth,
        (-3.0 * frac3 + 3.0 * frac2 + 3.0 * frac + 1.0) * sixth,
        frac3 * sixth,
    ]
    return moved >> 4, weights


def pack_kernel(sci_hbm, iv_hbm, taps_hbm, out_ref, sci_ref, iv_ref, taps_ref, sems):
    copies = [
        pltpu.make_async_copy(src, dst, sems.at[i])
        for i, (src, dst) in enumerate(
            [(sci_hbm, sci_ref), (iv_hbm, iv_ref), (taps_hbm, taps_ref)]
        )
    ]
    for copy in copies:
        copy.start()
    for copy in copies:
        copy.wait()
    rows, cols = sci_ref.shape[1:]
    iv = iv_ref[0]
    out_ref[0:rows, :] = (sci_ref[0] * iv).astype(jnp.bfloat16)
    out_ref[rows : 2 * rows, :] = iv.astype(jnp.bfloat16)
    taps = taps_ref[...]
    p = taps / jnp.sum(taps, axis=1, keepdims=True)
    p = jnp.concatenate([p, jnp.zeros((1, cols - p.shape[1]), jnp.float32)], axis=1)
    hi = p.astype(jnp.bfloat16).astype(jnp.float32)
    mid = (p - hi).astype(jnp.bfloat16).astype(jnp.float32)
    low = p - hi - mid
    row = lax.broadcasted_iota(jnp.int32, (16, cols), 0)
    block = jnp.where(row == 0, hi, jnp.where(row == 1, mid, jnp.where(row == 2, low, 0.0)))
    out_ref[2 * rows :, :] = block.astype(jnp.bfloat16)


def strip_kernel(rows, place_ref, own_ref, a_ref, b_ref):
    odd = place_ref[4] > 0
    heads, tails = [], []
    for i in range(2):
        x = own_ref[i * rows : (i + 1) * rows, :].astype(jnp.float32)
        heads.append(x[:RIM])
        tails.append(x[rows - RIM :])
    head = jnp.concatenate(heads, 0)
    tail = jnp.concatenate(tails, 0)
    a_ref[...] = jnp.where(odd, head, tail).astype(jnp.bfloat16)
    b_ref[...] = jnp.where(odd, tail, head).astype(jnp.bfloat16)


def turned(pieces, by):
    count = len(pieces)
    whole, part = divmod(by, 128)
    near = pieces[-whole % count]
    if part == 0:
        return near
    far = pieces[(-whole - 1) % count]
    lane = lax.broadcasted_iota(jnp.int32, near.shape, 1)
    return jnp.where(lane >= part, pltpu.roll(near, part, 1), pltpu.roll(far, part, 1))


def select(d, weights):
    acc = jnp.zeros(d.shape, jnp.float32)
    for a, w in enumerate(weights):
        acc = jnp.where(d == a, w, acc)
    return acc


def shift_kernel(hyps, rows, all_cols, place_ref, base_ref, times_ref, speed_ref, rb_ref, cb_ref):
    circle = rb_ref.shape[2]
    r = lax.broadcasted_iota(jnp.int32, (8, circle), 0)
    k = lax.broadcasted_iota(jnp.int32, (8, circle), 1)
    row_base = k - r
    r = lax.broadcasted_iota(jnp.int32, (8, all_cols), 0)
    m = lax.broadcasted_iota(jnp.int32, (8, all_cols), 1)
    col_base = r - m

    def one(e, carry):
        time = times_ref[place_ref[2] ^ (base_ref[0] + e)]
        for h in range(hyps):
            whole, weights = spline_taps(speed_ref[h, 0], time)
            base = select((row_base - (whole - 1)) & (circle - 1), weights)
            pieces = [base[:, j : j + 128] for j in range(0, circle, 128)]
            turns = [pieces[-j:] + pieces[:-j] for j in range(len(pieces), 0, -1)]
            blocks = [
                jnp.concatenate([turned(turn, n) for turn in turns], 1) for n in range(0, rows, 8)
            ]
            rb_ref[e, h * rows : (h + 1) * rows, :] = jnp.concatenate(blocks, 0).astype(jnp.bfloat16)
            whole, weights = spline_taps(speed_ref[h, 1], time)
            d = col_base - (whole - 1)
            base = select(jnp.where(d < 0, d + all_cols, d), weights)
            pieces = [base[:, j : j + 128] for j in range(0, all_cols, 128)]
            cb_ref[h, e] = jnp.concatenate(
                [turned(pieces, n) for n in range(0, all_cols, 8)], 0
            ).astype(jnp.bfloat16)
        return carry

    lax.fori_loop(0, rb_ref.shape[0], one, 0)


def blur_kernel(rows, cols, place_ref, tile_ref, br_ref, bc_ref):
    out_rows = br_ref.shape[1]
    all_cols = bc_ref.shape[1]
    low_row = place_ref[0]
    high_row = place_ref[1]
    odd = place_ref[4]
    first_a = jnp.where(odd > 0, -RIM, rows)
    first_b = jnp.where(odd > 0, rows, -RIM)
    block = tile_ref[2 * rows : 2 * rows + 16, :].astype(jnp.float32)
    p = block[0:1] + block[1:2] + block[2:3]
    kernels = (p, p * p)

    def fill(d, images):
        found = [jnp.zeros(d.shape, jnp.float32)] * len(images)
        for t in range(2 * PR + 1):
            hit = d == t
            for at, i in enumerate(images):
                found[at] = jnp.where(hit, kernels[i][:, t : t + 1], found[at])
        return found

    zero = jnp.zeros((16, 128), jnp.float32)
    for n0 in range(0, out_rows, 16):
        start = n0 if n0 < rows + REACH else n0 - out_rows
        n = lax.broadcasted_iota(jnp.int32, (16, 128), 0) + start
        inside = (n >= low_row) & (n < high_row)
        k = lax.broadcasted_iota(jnp.int32, (16, 128), 1)
        tile = [zero, zero]
        if start + 16 + PR > 0 and start - PR < rows:
            tile = fill(jnp.where(inside, k - n + PR, -1), (0, 1))
        for i in range(2):
            rim = zero
            if start + 16 + PR > rows or start - PR < 0:
                w = k + 16 * i
                c = jnp.where(
                    (w >= i * RIM) & (w < (i + 1) * RIM),
                    first_a + w - i * RIM,
                    jnp.where(
                        (w >= (2 + i) * RIM) & (w < (3 + i) * RIM),
                        first_b + w - (2 + i) * RIM,
                        -4096,
                    ),
                )
                rim = fill(jnp.where(inside, c - n + PR, -1), (i,))[0]
            br_ref[i, n0 : n0 + 16, :] = jnp.concatenate([tile[i], rim], 1).astype(jnp.bfloat16)
    r = lax.broadcasted_iota(jnp.int32, (8, all_cols), 0)
    m = lax.broadcasted_iota(jnp.int32, (8, all_cols), 1)
    d = r - m + PR
    for i, base in enumerate(fill(jnp.where(d < 0, d + all_cols, d), (0, 1))):
        pieces = [base[:, j : j + 128] for j in range(0, all_cols, 128)]
        bc_ref[i] = jnp.concatenate(
            [turned(pieces, n) for n in range(0, all_cols, 8)], 0
        ).astype(jnp.bfloat16)


def dot(a, b):
    return jnp.dot(a, b, preferred_element_type=jnp.float32)


def widen(c, count):
    total = c.shape[0]
    return jnp.concatenate(
        [c] + [jnp.concatenate([c[total - 128 * j :], c[: total - 128 * j]], 0) for j in range(1, count)],
        1,
    )


def stack_kernel(slot, hyps, rows, cols, first, final, place_ref, *refs):
    refs = list(refs)
    tile, halo, side_tile, side_halo, br, bc, rb, cb = refs[:8]
    acc = None if first else refs[8]
    out = refs[-1]
    out_rows = br.shape[1]
    wide = cols + 128
    lane = lax.broadcasted_iota(jnp.int32, (1, 128), 1)
    after = jnp.where((lane < 64) & (place_ref[5] > 0), 1.0, 0.0)
    before = jnp.where((lane >= 64) & (place_ref[6] > 0), 1.0, 0.0)
    side = (after + before).astype(jnp.bfloat16)
    after = after.astype(jnp.bfloat16)
    before = before.astype(jnp.bfloat16)
    unused = jnp.zeros((out_rows - rows - 2 * REACH, wide), jnp.float32)
    upper = rows + REACH
    pair = []
    for i in range(2):
        at = slice(i * rows, (i + 1) * rows)
        rim = slice(16 * i, 16 * i + 128)
        left = jnp.concatenate([tile[at, :], halo[rim, :]], 0)
        right = jnp.concatenate([side_tile[at, :], side_halo[rim, :]], 0)
        right = right[:, :128] * after + right[:, cols - 128 :] * before
        field = jnp.concatenate([left, right], 1)
        half = jnp.concatenate([br[i, :upper, :], br[i, out_rows - REACH :, :]], 0)
        half = dot(half, field).astype(jnp.bfloat16)
        image = dot(half, widen(bc[i], wide // 128))
        image = jnp.concatenate([image[:upper], unused, image[upper:]], 0).astype(jnp.bfloat16)
        pair += [image[:, :cols], image[:, cols:] * side]
    moved = dot(rb[slot], jnp.concatenate(pair, 1)).astype(jnp.bfloat16)
    for h in range(hyps):
        at = slice(h * rows, (h + 1) * rows)
        both = jnp.concatenate([moved[at, :wide], moved[at, wide:]], 0)
        total = dot(both, widen(cb[h, slot], cols // 128))
        if not first:
            total = total + acc[h]
        if final:
            out[h] = total[:rows] / jnp.sqrt(total[rows:])
        else:
            out[h] = total


VMEM = pl.BlockSpec(memory_space=pltpu.VMEM)
SMEM = pl.BlockSpec(memory_space=pltpu.SMEM)
PARAMS = pltpu.CompilerParams(vmem_limit_bytes=VMEM_LIMIT)


def call(kernel, specs, shapes, *args, scratch=(), flops=0, bytes_accessed=0):
    single = not isinstance(shapes, (list, tuple))
    return pl.pallas_call(
        kernel,
        out_shape=shapes,
        in_specs=specs,
        out_specs=VMEM if single else [VMEM] * len(shapes),
        scratch_shapes=list(scratch),
        compiler_params=PARAMS,
        cost_estimate=pl.CostEstimate(
            flops=flops, bytes_accessed=bytes_accessed, transcendentals=0
        ),
    )(*args)


def bf16(*shape):
    return jax.ShapeDtypeStruct(shape, jnp.bfloat16)


def side_swap(x):
    count = lax.axis_size("ty")
    if count == 2:
        return lax.ppermute(x, "ty", [(0, 1), (1, 0)])
    after = lax.ppermute(x[:, :128], "ty", [(i + 1, i) for i in range(count - 1)])
    before = lax.ppermute(x[:, x.shape[1] - 128 :], "ty", [(i, i + 1) for i in range(count - 1)])
    return jnp.concatenate([after, before], 1)


def shards(science, inv_variance, psf_taps, epoch_times, velocities):
    rows, cols = science.shape[1:]
    hyps = velocities.shape[0]
    epochs = lax.axis_size("ea")
    tx = lax.axis_size("tx")
    ty = lax.axis_size("ty")
    here_x = lax.axis_index("tx")
    here_y = lax.axis_index("ty")
    here_e = lax.axis_index("ea")
    all_cols = cols + 128
    slots = min(GROUP, epochs)

    place = jnp.stack(
        [
            jnp.where(here_x == 0, 0, -REACH),
            jnp.where(here_x == tx - 1, rows, rows + REACH),
            here_e,
            here_x,
            here_x % 2,
            jnp.where(here_y < ty - 1, 1, 0),
            jnp.where(here_y > 0, 1, 0),
        ]
    ).astype(jnp.int32)

    own = call(
        pack_kernel,
        [pl.BlockSpec(memory_space=pltpu.HBM)] * 3,
        bf16(2 * rows + 16, cols),
        science,
        inv_variance,
        psf_taps,
        scratch=[
            pltpu.VMEM(science.shape, jnp.float32),
            pltpu.VMEM(science.shape, jnp.float32),
            pltpu.VMEM(psf_taps.shape, jnp.float32),
            pltpu.SemaphoreType.DMA((3,)),
        ],
    )
    tiles = [own] + [
        lax.ppermute(own, "ea", [(i, i ^ k) for i in range(epochs)]) for k in range(1, epochs)
    ]
    strip_a, strip_b = call(
        functools.partial(strip_kernel, rows),
        [SMEM, VMEM],
        [bf16(2 * RIM, cols)] * 2,
        place,
        own,
        flops=STRIP_FLOPS,
    )
    swap_b = [(i, i + 1) for i in range(1, tx - 1, 2)] + [(i + 1, i) for i in range(1, tx - 1, 2)]
    swap_a = [(i, i + 1) for i in range(0, tx - 1, 2)] + [(i + 1, i) for i in range(0, tx - 1, 2)]
    rim_b = lax.ppermute(strip_b, "tx", swap_b)
    rim_a = lax.ppermute(strip_a, "tx", swap_a)
    halo = jnp.concatenate([rim_a, rim_b], 0)
    def shift_bands(base):
        return call(
            functools.partial(shift_kernel, hyps, rows, all_cols),
            [SMEM] * 4,
            [bf16(slots, hyps * rows, 2 * rows), bf16(hyps, slots, all_cols, 128)],
            place,
            base,
            epoch_times,
            velocities,
            flops=SHIFT_FLOPS,
        )

    def blur_bands(tile):
        return call(
            functools.partial(blur_kernel, rows, cols),
            [SMEM, VMEM],
            [bf16(2, 2 * rows, 2 * rows), bf16(2, all_cols, 128)],
            place,
            tile,
            flops=BLUR_FLOPS,
        )

    def stack(slot, tile, halo, blurs, shifts, total, final):
        args = [place, tile, halo, side_swap(tile), side_swap(halo), *blurs, *shifts]
        if total is not None:
            args.append(total)
        shape = (hyps, rows, cols) if final else (hyps, 2 * rows, cols)
        return call(
            functools.partial(stack_kernel, slot, hyps, rows, cols, total is None, final),
            [SMEM] + [VMEM] * (len(args) - 1),
            jax.ShapeDtypeStruct(shape, jnp.float32),
            *args,
            flops=STACK_FLOPS,
        )

    if epochs == slots:
        shifts = shift_bands(jnp.zeros((1,), jnp.int32))
        blurs = [blur_bands(tile) for tile in tiles]
        *shifts, halo = lax.optimization_barrier((*shifts, halo))
        halos = [halo]
        for k in range(1, epochs):
            *blurs[k], sent = lax.optimization_barrier((*blurs[k], halo))
            halos.append(lax.ppermute(sent, "ea", [(i, i ^ k) for i in range(epochs)]))
        total = None
        order = [0, *range(epochs - 1, 0, -1)]
        for k in order:
            total = stack(k, tiles[k], halos[k], blurs[k], shifts, total, k == order[-1])
        return total

    halos = [halo] + [
        lax.ppermute(halo, "ea", [(i, i ^ k) for i in range(epochs)]) for k in range(1, epochs)
    ]

    def step(total, xs):
        tiles, halos, base = xs
        shifts = shift_bands(base)
        for k in range(slots):
            total = stack(k, tiles[k], halos[k], blur_bands(tiles[k]), shifts, total, False)
        return total, None

    split = lambda x: x.reshape((epochs // slots, slots) + x.shape[1:])
    zeros = jnp.zeros((hyps, 2 * rows, cols), jnp.float32)
    bases = jnp.arange(0, epochs, slots, dtype=jnp.int32)[:, None]
    every = (split(jnp.stack(tiles)), split(jnp.stack(halos)), bases)
    total, _ = lax.scan(step, zeros, every)
    return total[:, :rows] / jnp.sqrt(total[:, rows:])


def solution(mesh):
    in_specs = (P("ea", "tx", "ty"), P("ea", "tx", "ty"), P("ea", None), P(), P("ea", None))
    out_specs = P("ea", "tx", "ty")
    return jax.shard_map(shards, mesh=mesh, in_specs=in_specs, out_specs=out_specs, check_vma=False)
```

```python
import functools

import jax
import jax.numpy as jnp
from jax import lax
from jax.experimental import pallas as pl
from jax.experimental.pallas import tpu as pltpu
from jax.sharding import PartitionSpec as P

REACH = 32
PR = 4
RIM = REACH + PR
GROUP = 4
VMEM_LIMIT = 24 * 1024 * 1024
STRIP_FLOPS = 10_000_000
SHIFT_FLOPS = 4_000_000_000
BLUR_FLOPS = 4_000_000_000
STACK_FLOPS = 2_000_000_000


def spline_taps(speed, time):
    moved = (speed * time) >> 3
    frac = (moved & 15).astype(jnp.float32) * (1.0 / 16.0)
    rest = 1.0 - frac
    frac2 = frac * frac
    frac3 = frac2 * frac
    sixth = 1.0 / 6.0
    weights = [
        rest * rest * rest * sixth,
        (3.0 * frac3 - 6.0 * frac2 + 4.0) * sixth,
        (-3.0 * frac3 + 3.0 * frac2 + 3.0 * frac + 1.0) * sixth,
        frac3 * sixth,
    ]
    return moved >> 4, weights


def packed(science, inv_variance, psf_taps):
    cols = science.shape[2]
    taps = jnp.broadcast_to(jnp.pad(psf_taps, ((0, 0), (0, cols - psf_taps.shape[1]))), (16, cols))
    hi = lax.reduce_precision(taps, 8, 7)
    mid = lax.reduce_precision(taps - hi, 8, 7)
    row = lax.broadcasted_iota(jnp.int32, (16, cols), 0)
    taps = jnp.where(row == 0, hi, jnp.where(row == 1, mid, taps - hi - mid))
    return jnp.concatenate([science[0] * inv_variance[0], inv_variance[0], taps], 0).astype(jnp.bfloat16)


def strip_kernel(rows, own_ref, a_ref, b_ref):
    odd = lax.axis_index("tx") % 2 > 0
    heads, tails = [], []
    for i in range(2):
        x = own_ref[i * rows : (i + 1) * rows, :].astype(jnp.float32)
        heads.append(x[:RIM])
        tails.append(x[rows - RIM :])
    head = jnp.concatenate(heads, 0)
    tail = jnp.concatenate(tails, 0)
    a_ref[...] = jnp.where(odd, head, tail).astype(jnp.bfloat16)
    b_ref[...] = jnp.where(odd, tail, head).astype(jnp.bfloat16)


def turned(pieces, by):
    count = len(pieces)
    whole, part = divmod(by, 128)
    near = pieces[-whole % count]
    if part == 0:
        return near
    far = pieces[(-whole - 1) % count]
    lane = lax.broadcasted_iota(jnp.int32, near.shape, 1)
    return jnp.where(lane >= part, pltpu.roll(near, part, 1), pltpu.roll(far, part, 1))


def cut(base):
    return [base[:, j : j + 128] for j in range(0, base.shape[1], 128)]


def select(d, weights):
    acc = jnp.zeros(d.shape, jnp.float32)
    for a, w in enumerate(weights):
        acc = jnp.where(d == a, w, acc)
    return acc.astype(jnp.bfloat16)


def distance(count, source_axis):
    d = lax.broadcasted_iota(jnp.int32, (16, count), source_axis) - lax.broadcasted_iota(
        jnp.int32, (16, count), 1 - source_axis
    )
    return d


def shift_kernel(hyps, rows, all_cols, base_ref, times_ref, speed_ref, rb_ref, cb_ref):
    circle = rb_ref.shape[2]
    row_base = distance(circle, 1)
    col_base = distance(all_cols, 0)

    def one(e, carry):
        time = times_ref[lax.axis_index("ea") ^ (base_ref[0] + e)]
        for h in range(hyps):
            whole, weights = spline_taps(speed_ref[h, 0], time)
            pieces = cut(select((row_base - (whole - 1)) & (circle - 1), weights))
            turns = [pieces[-j:] + pieces[:-j] for j in range(len(pieces), 0, -1)]
            for n in range(0, rows, 16):
                for j, turn in enumerate(turns):
                    rb_ref[e, h * rows + n : h * rows + n + 16, 128 * j : 128 * (j + 1)] = turned(turn, n)
            whole, weights = spline_taps(speed_ref[h, 1], time)
            d = col_base - (whole - 1)
            pieces = cut(select(jnp.where(d < 0, d + all_cols, d), weights))
            for n in range(0, all_cols, 16):
                cb_ref[h, e, n : n + 16, :] = turned(pieces, n)
        return carry

    lax.fori_loop(0, rb_ref.shape[0], one, 0)


def blur_kernel(rows, cols, last_x, tile_ref, br_ref, bc_ref):
    out_rows, circle = br_ref.shape[1:]
    all_cols = bc_ref.shape[1]
    here_x = lax.axis_index("tx")
    odd = here_x % 2 > 0
    one = jnp.ones((16, 128), jnp.float32)
    keep_above = jnp.where(here_x > 0, one, 0.0).astype(jnp.bfloat16)
    keep_below = jnp.where(here_x < last_x, one, 0.0).astype(jnp.bfloat16)
    block = tile_ref[2 * rows : 2 * rows + 16, :].astype(jnp.float32)
    p = block[0:1] + block[1:2] + block[2:3]
    p = p / jnp.sum(p, axis=1, keepdims=True)
    taps = [p[:, t : t + 1] for t in range(2 * PR + 1)]
    kernels = (taps, [t * t for t in taps])
    row_base = (distance(circle, 1) + PR) & (circle - 1)
    col_base = distance(all_cols, 0) + PR
    col_base = jnp.where(col_base < 0, col_base + all_cols, col_base)
    lane = lax.broadcasted_iota(jnp.int32, (16, 128), 1)
    for i in range(2):
        pieces = cut(select(row_base, kernels[i]))
        first_a = (RIM - 16) * i
        first_b = 2 * RIM + first_a

        def rim(n, lanes, coordinate):
            return jnp.where(
                (lane >= lanes) & (lane < lanes + RIM), turned(pieces, (n + lanes - coordinate) % circle), 0.0
            ).astype(jnp.bfloat16)

        for at in range(0, out_rows, 16):
            n = at if at < rows + REACH else at - out_rows
            left = turned(pieces, n % circle)
            right = jnp.zeros((16, 128), jnp.bfloat16)
            if n - PR < 0:
                right = jnp.where(odd, rim(n, first_a, -RIM), rim(n, first_b, -RIM))
            elif n + 16 + PR > rows:
                right = jnp.where(odd, rim(n, first_b, rows), rim(n, first_a, rows))
            if n < 0 or n >= rows:
                keep = keep_above if n < 0 else keep_below
                left, right = left * keep, right * keep
            br_ref[i, at : at + 16, :128] = left
            br_ref[i, at : at + 16, 128:] = right
        pieces = cut(select(col_base, kernels[i]))
        for n in range(0, all_cols, 16):
            bc_ref[i, n : n + 16, :] = turned(pieces, n)


def dot(a, b):
    return jnp.dot(a, b, preferred_element_type=jnp.float32)


def widen(c, count):
    total = c.shape[0]
    return jnp.concatenate(
        [c] + [jnp.concatenate([c[total - 128 * j :], c[: total - 128 * j]], 0) for j in range(1, count)],
        1,
    )


def stack_kernel(slots, hyps, rows, cols, last_y, first, final, spots, *refs):
    count = len(slots)
    refs = list(refs)
    tiles, halos, brs, bcs = [[refs.pop(0) for _ in range(count)] for _ in range(4)]
    side_tiles, side_halos, rb, cb = [refs.pop(0) for _ in range(4)]
    acc = None if first else refs.pop(0)
    out = refs.pop(0)
    wide = cols + 128
    lane = lax.broadcasted_iota(jnp.int32, (1, 128), 1)
    here_y = lax.axis_index("ty")
    after = jnp.where((lane < 64) & (here_y < last_y), 1.0, 0.0)
    before = jnp.where((lane >= 64) & (here_y > 0), 1.0, 0.0)
    side = (after + before).astype(jnp.bfloat16)
    after = after.astype(jnp.bfloat16)
    before = before.astype(jnp.bfloat16)
    upper = rows + REACH
    unused = jnp.zeros((rb.shape[2] - rows - 2 * REACH, wide), jnp.float32)
    moved = []
    for j in range(count):
        pair = []
        tile_at, halo_at = spots[j]
        for i in range(2):
            at = i * rows
            rim = 16 * i
            left = jnp.concatenate([tiles[j][at : at + rows, :], halos[j][rim : rim + 128, :]], 0)
            right = [
                side_tiles[tile_at + at : tile_at + at + rows, :],
                side_halos[halo_at + rim : halo_at + rim + 128, :],
            ]
            right = jnp.concatenate(right, 0)
            right = right[:, :128] * after + right[:, cols - 128 :] * before
            half = dot(brs[j][i], jnp.concatenate([left, right], 1)).astype(jnp.bfloat16)
            image = dot(half, widen(bcs[j][i], wide // 128))
            image = jnp.concatenate([image[:upper], unused, image[upper:]], 0).astype(jnp.bfloat16)
            pair += [image[:, :cols], image[:, cols:] * side]
        moved.append(dot(rb[slots[j]], jnp.concatenate(pair, 1)).astype(jnp.bfloat16))
    copies = []
    for h in range(hyps):
        at = slice(h * rows, (h + 1) * rows)
        both = [jnp.concatenate([m[at, :wide], m[at, wide:]], 0) for m in moved]
        bands = [widen(cb[h, k], cols // 128) for k in slots]
        total = dot(jnp.concatenate(both, 1), jnp.concatenate(bands, 0))
        if not first:
            total = total + acc[h]
        if final:
            held, sems = refs
            held[h] = total[:rows] * lax.rsqrt(total[rows:])
            copies.append(pltpu.make_async_copy(held.at[h], out.at[h], sems.at[h]))
            copies[-1].start()
        else:
            out[h] = total
    for copy in copies:
        copy.wait()


VMEM = pl.BlockSpec(memory_space=pltpu.VMEM)
SMEM = pl.BlockSpec(memory_space=pltpu.SMEM)
PARAMS = pltpu.CompilerParams(vmem_limit_bytes=VMEM_LIMIT)


def call(kernel, specs, shapes, *args, scratch=(), flops=0, out=VMEM):
    single = not isinstance(shapes, (list, tuple))
    return pl.pallas_call(
        kernel,
        out_shape=shapes,
        in_specs=specs,
        out_specs=out if single else [out] * len(shapes),
        scratch_shapes=list(scratch),
        compiler_params=PARAMS,
        cost_estimate=pl.CostEstimate(flops=flops, bytes_accessed=0, transcendentals=0),
    )(*args)


def bf16(*shape):
    return jax.ShapeDtypeStruct(shape, jnp.bfloat16)


def side_swap(x):
    count = lax.axis_size("ty")
    if count == 2:
        return lax.ppermute(x, "ty", [(0, 1), (1, 0)])
    after = lax.ppermute(x[:, :128], "ty", [(i + 1, i) for i in range(count - 1)])
    before = lax.ppermute(x[:, x.shape[1] - 128 :], "ty", [(i, i + 1) for i in range(count - 1)])
    return jnp.concatenate([after, before], 1)


def shards(science, inv_variance, psf_taps, epoch_times, velocities):
    rows, cols = science.shape[1:]
    hyps = velocities.shape[0]
    epochs = lax.axis_size("ea")
    tx = lax.axis_size("tx")
    ty = lax.axis_size("ty")
    all_cols = cols + 128
    slots = min(GROUP, epochs)

    own = packed(science, inv_variance, psf_taps)
    tiles = [own] + [
        lax.ppermute(own, "ea", [(i, i ^ k) for i in range(epochs)]) for k in range(1, epochs)
    ]
    cut_from = own
    if epochs == slots:
        pass
    strip_a, strip_b = call(
        functools.partial(strip_kernel, rows),
        [VMEM],
        [bf16(2 * RIM, cols)] * 2,
        cut_from,
        flops=STRIP_FLOPS,
    )
    swap_b = [(i, i + 1) for i in range(1, tx - 1, 2)] + [(i + 1, i) for i in range(1, tx - 1, 2)]
    swap_a = [(i, i + 1) for i in range(0, tx - 1, 2)] + [(i + 1, i) for i in range(0, tx - 1, 2)]
    rim_b = lax.ppermute(strip_b, "tx", swap_b)
    rim_a = lax.ppermute(strip_a, "tx", swap_a)
    halo = jnp.concatenate([rim_a, rim_b], 0)
    def shift_bands(base):
        return call(
            functools.partial(shift_kernel, hyps, rows, all_cols),
            [SMEM] * 3,
            [bf16(slots, hyps * rows, 2 * rows), bf16(hyps, slots, all_cols, 128)],
            base,
            epoch_times,
            velocities,
            flops=SHIFT_FLOPS,
        )

    def blur_bands(tile):
        return call(
            functools.partial(blur_kernel, rows, cols, tx - 1),
            [VMEM],
            [bf16(2, rows + 2 * REACH, 2 * rows), bf16(2, all_cols, 128)],
            tile,
            flops=BLUR_FLOPS,
        )

    def stack(slots, tiles, halos, blurs, side_tiles, side_halos, shifts, total, final):
        args = [*tiles, *halos, *[x[0] for x in blurs], *[x[1] for x in blurs], side_tiles, side_halos, *shifts]
        if total is not None:
            args.append(total)
        shape = (hyps, rows, cols) if final else (hyps, 2 * rows, cols)
        shape = jax.ShapeDtypeStruct(shape, jnp.float32)
        spots = [(j * own.shape[0], j * halo.shape[0]) for j in range(len(slots))]
        return call(
            functools.partial(
                stack_kernel, slots, hyps, rows, cols, ty - 1, total is None, final, spots
            ),
            [VMEM] * len(args),
            shape,
            *args,
            flops=STACK_FLOPS,
            out=pl.BlockSpec(memory_space=pltpu.HBM) if final else VMEM,
            scratch=[pltpu.VMEM(shape.shape, jnp.float32), pltpu.SemaphoreType.DMA((hyps,))] if final else [],
        )

    def beside(arrays):
        return side_swap(jnp.concatenate(arrays, 0))

    if epochs == slots:
        shifts = shift_bands(jnp.zeros((1,), jnp.int32))
        *shifts, halo = lax.optimization_barrier((*shifts, halo))
        halos = [halo] + [
            lax.ppermute(halo, "ea", [(i, i ^ k) for i in range(epochs)]) for k in range(1, epochs)
        ]
        side = beside([own, halo])
        total = stack([0], [own], [halo], [blur_bands(own)], side[: own.shape[0]], side[own.shape[0] :], shifts, None, False)
        taken = [1, 3, 2]
        total, *others = lax.optimization_barrier((total, *[tiles[k] for k in taken]))
        others = [others[taken.index(k)] for k in range(1, epochs)]
        blurs = [blur_bands(x) for x in others]
        later = beside(others)
        flat = [x for pair in blurs for x in pair]
        taken = [1, 3, 2]
        total, later, *rest = lax.optimization_barrier((total, later, *flat, *[halos[k] for k in taken]))
        blurs = [rest[2 * j : 2 * j + 2] for j in range(epochs - 1)]
        rims = rest[2 * (epochs - 1) :]
        rims = [rims[taken.index(k)] for k in range(1, epochs)]
        return stack(list(range(1, epochs)), others, rims, blurs, later, beside(rims), shifts, total, True)

    halos = [halo] + [
        lax.ppermute(halo, "ea", [(i, i ^ k) for i in range(epochs)]) for k in range(1, epochs)
    ]

    def step(total, xs):
        tiles, halos, base = xs
        tiles = [tiles[k] for k in range(slots)]
        halos = [halos[k] for k in range(slots)]
        blurs = [blur_bands(x) for x in tiles]
        shifts = shift_bands(base)
        return stack(list(range(slots)), tiles, halos, blurs, beside(tiles), beside(halos), shifts, total, False), None

    split = lambda x: x.reshape((epochs // slots, slots) + x.shape[1:])
    zeros = jnp.zeros((hyps, 2 * rows, cols), jnp.float32)
    bases = jnp.arange(0, epochs, slots, dtype=jnp.int32)[:, None]
    every = (split(jnp.stack(tiles)), split(jnp.stack(halos)), bases)
    total, _ = lax.scan(step, zeros, every)
    return total[:, :rows] / jnp.sqrt(total[:, rows:])


def solution(mesh):
    in_specs = (P("ea", "tx", "ty"), P("ea", "tx", "ty"), P("ea", None), P(), P("ea", None))
    out_specs = P("ea", "tx", "ty")
    return jax.shard_map(shards, mesh=mesh, in_specs=in_specs, out_specs=out_specs, check_vma=False)
```

```python
import functools

import jax
import jax.numpy as jnp
from jax import lax
from jax.experimental import pallas as pl
from jax.experimental.pallas import tpu as pltpu
from jax.sharding import PartitionSpec as P

REACH = 32
PR = 4
RIM = REACH + PR
GROUP = 4
VMEM_LIMIT = 24 * 1024 * 1024
STRIP_FLOPS = 10_000_000
SHIFT_FLOPS = 4_000_000_000
BLUR_FLOPS = 4_000_000_000
STACK_FLOPS = 2_000_000_000


def spline_taps(speed, time):
    moved = (speed * time) >> 3
    frac = (moved & 15).astype(jnp.float32) * (1.0 / 16.0)
    rest = 1.0 - frac
    frac2 = frac * frac
    frac3 = frac2 * frac
    sixth = 1.0 / 6.0
    weights = [
        rest * rest * rest * sixth,
        (3.0 * frac3 - 6.0 * frac2 + 4.0) * sixth,
        (-3.0 * frac3 + 3.0 * frac2 + 3.0 * frac + 1.0) * sixth,
        frac3 * sixth,
    ]
    return moved >> 4, weights


def strip_kernel(rows, own_ref, a_ref, b_ref):
    odd = lax.axis_index("tx") % 2 > 0
    heads, tails = [], []
    for i in range(2):
        x = own_ref[i * rows : (i + 1) * rows, :].astype(jnp.float32)
        heads.append(x[:RIM])
        tails.append(x[rows - RIM :])
    head = jnp.concatenate(heads, 0)
    tail = jnp.concatenate(tails, 0)
    a_ref[...] = jnp.where(odd, head, tail).astype(jnp.bfloat16)
    b_ref[...] = jnp.where(odd, tail, head).astype(jnp.bfloat16)


SPARE = ((0, RIM - 1), (RIM, 2 * RIM - 1), (3 * RIM - 1, 2 * RIM))


def rim_kernel(taps_ref, a_ref, b_ref, out_ref):
    odd = lax.axis_index("tx") % 2 > 0
    cols = out_ref.shape[1]
    taps = taps_ref[...]
    taps = jnp.concatenate([taps, jnp.zeros((1, cols - taps.shape[1]), jnp.float32)], 1)
    hi = taps.astype(jnp.bfloat16).astype(jnp.float32)
    mid = (taps - hi).astype(jnp.bfloat16).astype(jnp.float32)
    rims = jnp.concatenate([a_ref[...].astype(jnp.float32), b_ref[...].astype(jnp.float32)], 0)
    row = lax.broadcasted_iota(jnp.int32, rims.shape, 0)
    for (on_odd, on_even), part in zip(SPARE, (hi, mid, taps - hi - mid)):
        rims = jnp.where(row == jnp.where(odd, on_odd, on_even), part, rims)
    out_ref[...] = rims.astype(jnp.bfloat16)


def turned(pieces, by):
    count = len(pieces)
    whole, part = divmod(by, 128)
    near = pieces[-whole % count]
    if part == 0:
        return near
    far = pieces[(-whole - 1) % count]
    lane = lax.broadcasted_iota(jnp.int32, near.shape, 1)
    return jnp.where(lane >= part, pltpu.roll(near, part, 1), pltpu.roll(far, part, 1))


def cut(base):
    return [base[:, j : j + 128] for j in range(0, base.shape[1], 128)]


def select(d, weights):
    acc = jnp.zeros(d.shape, jnp.float32)
    for a, w in enumerate(weights):
        acc = jnp.where(d == a, w, acc)
    return acc.astype(jnp.bfloat16)


def distance(count, source_axis):
    d = lax.broadcasted_iota(jnp.int32, (16, count), source_axis) - lax.broadcasted_iota(
        jnp.int32, (16, count), 1 - source_axis
    )
    return d


def shift_kernel(hyps, rows, all_cols, base_ref, times_ref, speed_ref, rb_ref, cb_ref):
    circle = rb_ref.shape[2]
    row_base = distance(circle, 1)
    col_base = distance(all_cols, 0)

    def one(e, carry):
        time = times_ref[lax.axis_index("ea") ^ (base_ref[0] + e)]
        for h in range(hyps):
            whole, weights = spline_taps(speed_ref[h, 0], time)
            pieces = cut(select((row_base - (whole - 1)) & (circle - 1), weights))
            turns = [pieces[-j:] + pieces[:-j] for j in range(len(pieces), 0, -1)]
            for n in range(0, rows, 16):
                for j, turn in enumerate(turns):
                    rb_ref[e, h * rows + n : h * rows + n + 16, 128 * j : 128 * (j + 1)] = turned(turn, n)
            whole, weights = spline_taps(speed_ref[h, 1], time)
            d = col_base - (whole - 1)
            pieces = cut(select(jnp.where(d < 0, d + all_cols, d), weights))
            for n in range(0, all_cols, 16):
                cb_ref[h, e, n : n + 16, :] = turned(pieces, n)
        return carry

    lax.fori_loop(0, rb_ref.shape[0], one, 0)


def blur_kernel(rows, cols, last_x, *refs):
    count = len(refs) // 3
    for j in range(count):
        blur_one(rows, cols, last_x, refs[j], refs[count + 2 * j], refs[count + 2 * j + 1])


def blur_one(rows, cols, last_x, halo_ref, br_ref, bc_ref):
    out_rows, circle = br_ref.shape[1:]
    all_cols = bc_ref.shape[1]
    here_x = lax.axis_index("tx")
    odd = here_x % 2 > 0
    one = jnp.ones((16, 128), jnp.float32)
    keep_above = jnp.where(here_x > 0, one, 0.0).astype(jnp.bfloat16)
    keep_below = jnp.where(here_x < last_x, one, 0.0).astype(jnp.bfloat16)

    def held(row):
        block = halo_ref[row // 16 * 16 : row // 16 * 16 + 16, :].astype(jnp.float32)
        return block[row % 16 : row % 16 + 1]

    p = sum(jnp.where(odd, held(on_odd), held(on_even)) for on_odd, on_even in SPARE)
    p = p / jnp.sum(p, axis=1, keepdims=True)
    taps = [p[:, t : t + 1] for t in range(2 * PR + 1)]
    kernels = (taps, [t * t for t in taps])
    row_base = (distance(circle, 1) + PR) & (circle - 1)
    col_base = distance(all_cols, 0) + PR
    col_base = jnp.where(col_base < 0, col_base + all_cols, col_base)
    lane = lax.broadcasted_iota(jnp.int32, (16, 128), 1)
    for i in range(2):
        pieces = cut(select(row_base, kernels[i]))
        first_a = (RIM - 16) * i
        first_b = 2 * RIM + first_a

        def rim(n, lanes, coordinate):
            return jnp.where(
                (lane >= lanes) & (lane < lanes + RIM), turned(pieces, (n + lanes - coordinate) % circle), 0.0
            ).astype(jnp.bfloat16)

        for at in range(0, out_rows, 16):
            n = at if at < rows + REACH else at - out_rows
            left = turned(pieces, n % circle)
            right = jnp.zeros((16, 128), jnp.bfloat16)
            if n - PR < 0:
                right = jnp.where(odd, rim(n, first_a, -RIM), rim(n, first_b, -RIM))
            elif n + 16 + PR > rows:
                right = jnp.where(odd, rim(n, first_b, rows), rim(n, first_a, rows))
            if n < 0 or n >= rows:
                keep = keep_above if n < 0 else keep_below
                left, right = left * keep, right * keep
            br_ref[i, at : at + 16, :128] = left
            br_ref[i, at : at + 16, 128:] = right
        pieces = cut(select(col_base, kernels[i]))
        for n in range(0, all_cols, 16):
            bc_ref[i, n : n + 16, :] = turned(pieces, n)


def dot(a, b):
    return jnp.dot(a, b, preferred_element_type=jnp.float32)


def widen(c, count):
    total = c.shape[0]
    return jnp.concatenate(
        [c] + [jnp.concatenate([c[total - 128 * j :], c[: total - 128 * j]], 0) for j in range(1, count)],
        1,
    )


def stack_kernel(slots, hyps, rows, cols, last_y, first, final, spots, *refs):
    count = len(slots)
    refs = list(refs)
    tiles, halos, brs, bcs = [[refs.pop(0) for _ in range(count)] for _ in range(4)]
    side_tiles, side_halos, rb, cb = [refs.pop(0) for _ in range(4)]
    acc = None if first else refs.pop(0)
    out = refs.pop(0)
    wide = cols + 128
    lane = lax.broadcasted_iota(jnp.int32, (1, 128), 1)
    here_y = lax.axis_index("ty")
    after = jnp.where((lane < 64) & (here_y < last_y), 1.0, 0.0)
    before = jnp.where((lane >= 64) & (here_y > 0), 1.0, 0.0)
    side = (after + before).astype(jnp.bfloat16)
    after = after.astype(jnp.bfloat16)
    before = before.astype(jnp.bfloat16)
    upper = rows + REACH
    unused = jnp.zeros((rb.shape[2] - rows - 2 * REACH, wide), jnp.float32)
    moved = []
    for j in range(count):
        pair = []
        tile_at, halo_at = spots[j]
        for i in range(2):
            at = i * rows
            rim = 16 * i
            left = jnp.concatenate([tiles[j][at : at + rows, :], halos[j][rim : rim + 128, :]], 0)
            right = [
                side_tiles[tile_at + at : tile_at + at + rows, :],
                side_halos[halo_at + rim : halo_at + rim + 128, :],
            ]
            right = jnp.concatenate(right, 0)
            right = right[:, :128] * after + right[:, cols - 128 :] * before
            half = dot(brs[j][i], jnp.concatenate([left, right], 1)).astype(jnp.bfloat16)
            image = dot(half, widen(bcs[j][i], wide // 128))
            image = jnp.concatenate([image[:upper], unused, image[upper:]], 0).astype(jnp.bfloat16)
            pair += [image[:, :cols], image[:, cols:] * side]
        moved.append(dot(rb[slots[j]], jnp.concatenate(pair, 1)).astype(jnp.bfloat16))
    copies = []
    for h in range(hyps):
        at = slice(h * rows, (h + 1) * rows)
        both = [jnp.concatenate([m[at, :wide], m[at, wide:]], 0) for m in moved]
        bands = [widen(cb[h, k], cols // 128) for k in slots]
        total = dot(jnp.concatenate(both, 1), jnp.concatenate(bands, 0))
        if not first:
            total = total + acc[h]
        if final:
            held, sems = refs
            held[h] = total[:rows] * lax.rsqrt(total[rows:])
            copies.append(pltpu.make_async_copy(held.at[h], out.at[h], sems.at[h]))
            copies[-1].start()
        else:
            out[h] = total
    for copy in copies:
        copy.wait()


VMEM = pl.BlockSpec(memory_space=pltpu.VMEM)
SMEM = pl.BlockSpec(memory_space=pltpu.SMEM)
PARAMS = pltpu.CompilerParams(vmem_limit_bytes=VMEM_LIMIT)


def call(kernel, specs, shapes, *args, scratch=(), flops=0, out=VMEM):
    single = not isinstance(shapes, (list, tuple))
    return pl.pallas_call(
        kernel,
        out_shape=shapes,
        in_specs=specs,
        out_specs=out if single else [out] * len(shapes),
        scratch_shapes=list(scratch),
        compiler_params=PARAMS,
        cost_estimate=pl.CostEstimate(flops=flops, bytes_accessed=0, transcendentals=0),
    )(*args)


def bf16(*shape):
    return jax.ShapeDtypeStruct(shape, jnp.bfloat16)


def side_swap(x):
    count = lax.axis_size("ty")
    if count == 2:
        return lax.ppermute(x, "ty", [(0, 1), (1, 0)])
    after = lax.ppermute(x[:, :128], "ty", [(i + 1, i) for i in range(count - 1)])
    before = lax.ppermute(x[:, x.shape[1] - 128 :], "ty", [(i, i + 1) for i in range(count - 1)])
    return jnp.concatenate([after, before], 1)


def shards(science, inv_variance, psf_taps, epoch_times, velocities):
    rows, cols = science.shape[1:]
    hyps = velocities.shape[0]
    epochs = lax.axis_size("ea")
    tx = lax.axis_size("tx")
    ty = lax.axis_size("ty")
    all_cols = cols + 128
    slots = min(GROUP, epochs)

    own = jnp.concatenate([science[0] * inv_variance[0], inv_variance[0]], 0).astype(jnp.bfloat16)
    tiles = [own] + [
        lax.ppermute(own, "ea", [(i, i ^ k) for i in range(epochs)]) for k in range(1, epochs)
    ]
    cut_from = own
    if epochs == slots:
        pass
    strip_a, strip_b = call(
        functools.partial(strip_kernel, rows),
        [VMEM],
        [bf16(2 * RIM, cols)] * 2,
        cut_from,
        flops=STRIP_FLOPS,
    )
    swap_b = [(i, i + 1) for i in range(1, tx - 1, 2)] + [(i + 1, i) for i in range(1, tx - 1, 2)]
    swap_a = [(i, i + 1) for i in range(0, tx - 1, 2)] + [(i + 1, i) for i in range(0, tx - 1, 2)]
    rim_b = lax.ppermute(strip_b, "tx", swap_b)
    rim_a = lax.ppermute(strip_a, "tx", swap_a)
    halo = call(rim_kernel, [VMEM] * 3, bf16(4 * RIM, cols), psf_taps, rim_a, rim_b, flops=STRIP_FLOPS)
    def shift_bands(base):
        return call(
            functools.partial(shift_kernel, hyps, rows, all_cols),
            [SMEM] * 3,
            [bf16(slots, hyps * rows, 2 * rows), bf16(hyps, slots, all_cols, 128)],
            base,
            epoch_times,
            velocities,
            flops=SHIFT_FLOPS,
        )

    def blur_bands(halos):
        count = len(halos)
        bands = call(
            functools.partial(blur_kernel, rows, cols, tx - 1),
            [VMEM] * count,
            [bf16(2, rows + 2 * REACH, 2 * rows), bf16(2, all_cols, 128)] * count,
            *halos,
            flops=BLUR_FLOPS,
        )
        return [bands[2 * j : 2 * j + 2] for j in range(count)]

    def stack(slots, tiles, halos, blurs, side_tiles, side_halos, shifts, total, final):
        args = [*tiles, *halos, *[x[0] for x in blurs], *[x[1] for x in blurs], side_tiles, side_halos, *shifts]
        if total is not None:
            args.append(total)
        shape = (hyps, rows, cols) if final else (hyps, 2 * rows, cols)
        shape = jax.ShapeDtypeStruct(shape, jnp.float32)
        spots = [(j * own.shape[0], j * halo.shape[0]) for j in range(len(slots))]
        return call(
            functools.partial(
                stack_kernel, slots, hyps, rows, cols, ty - 1, total is None, final, spots
            ),
            [VMEM] * len(args),
            shape,
            *args,
            flops=STACK_FLOPS,
            out=pl.BlockSpec(memory_space=pltpu.HBM) if final else VMEM,
            scratch=[pltpu.VMEM(shape.shape, jnp.float32), pltpu.SemaphoreType.DMA((hyps,))] if final else [],
        )

    def beside(arrays):
        return side_swap(jnp.concatenate(arrays, 0))

    if epochs == slots:
        shifts = shift_bands(jnp.zeros((1,), jnp.int32))
        *shifts, halo = lax.optimization_barrier((*shifts, halo))
        halos = [halo] + [
            lax.ppermute(halo, "ea", [(i, i ^ k) for i in range(epochs)]) for k in range(1, epochs)
        ]
        side = beside([own, halo])
        total = stack([0], [own], [halo], blur_bands([halo]), side[: own.shape[0]], side[own.shape[0] :], shifts, None, False)
        taken = [1, 3, 2]
        others = lax.optimization_barrier([tiles[k] for k in taken])
        others = [others[taken.index(k)] for k in range(1, epochs)]
        later = beside(others)
        taken = [1, 3, 2]
        total, later, *rest = lax.optimization_barrier((total, later, *[halos[k] for k in taken]))
        rims = [rest[taken.index(k)] for k in range(1, epochs)]
        blurs = blur_bands(rims)
        return stack(list(range(1, epochs)), others, rims, blurs, later, beside(rims), shifts, total, True)

    halos = [halo] + [
        lax.ppermute(halo, "ea", [(i, i ^ k) for i in range(epochs)]) for k in range(1, epochs)
    ]

    def step(total, xs):
        tiles, halos, base = xs
        tiles = [tiles[k] for k in range(slots)]
        halos = [halos[k] for k in range(slots)]
        blurs = blur_bands(halos)
        shifts = shift_bands(base)
        return stack(list(range(slots)), tiles, halos, blurs, beside(tiles), beside(halos), shifts, total, False), None

    split = lambda x: x.reshape((epochs // slots, slots) + x.shape[1:])
    zeros = jnp.zeros((hyps, 2 * rows, cols), jnp.float32)
    bases = jnp.arange(0, epochs, slots, dtype=jnp.int32)[:, None]
    every = (split(jnp.stack(tiles)), split(jnp.stack(halos)), bases)
    total, _ = lax.scan(step, zeros, every)
    return total[:, :rows] / jnp.sqrt(total[:, rows:])


def solution(mesh):
    in_specs = (P("ea", "tx", "ty"), P("ea", "tx", "ty"), P("ea", None), P(), P("ea", None))
    out_specs = P("ea", "tx", "ty")
    return jax.shard_map(shards, mesh=mesh, in_specs=in_specs, out_specs=out_specs, check_vma=False)
```

```python
import functools

import jax
import jax.numpy as jnp
from jax import lax
from jax.experimental import pallas as pl
from jax.experimental.pallas import tpu as pltpu
from jax.sharding import PartitionSpec as P

REACH = 32
PR = 4
RIM = REACH + PR
GROUP = 4
VMEM_LIMIT = 24 * 1024 * 1024
STRIP_FLOPS = 10_000_000
SHIFT_FLOPS = 4_000_000_000
BLUR_FLOPS = 4_000_000_000
STACK_FLOPS = 2_000_000_000


def spline_taps(speed, time):
    moved = (speed * time) >> 3
    frac = (moved & 15).astype(jnp.float32) * (1.0 / 16.0)
    rest = 1.0 - frac
    frac2 = frac * frac
    frac3 = frac2 * frac
    sixth = 1.0 / 6.0
    weights = [
        rest * rest * rest * sixth,
        (3.0 * frac3 - 6.0 * frac2 + 4.0) * sixth,
        (-3.0 * frac3 + 3.0 * frac2 + 3.0 * frac + 1.0) * sixth,
        frac3 * sixth,
    ]
    return moved >> 4, weights


def strip_kernel(rows, own_ref, a_ref, b_ref):
    odd = lax.axis_index("tx") % 2 > 0
    heads, tails = [], []
    for i in range(2):
        x = own_ref[i * rows : (i + 1) * rows, :].astype(jnp.float32)
        heads.append(x[:RIM])
        tails.append(x[rows - RIM :])
    head = jnp.concatenate(heads, 0)
    tail = jnp.concatenate(tails, 0)
    a_ref[...] = jnp.where(odd, head, tail).astype(jnp.bfloat16)
    b_ref[...] = jnp.where(odd, tail, head).astype(jnp.bfloat16)


SPARE = ((0, RIM - 1), (RIM, 2 * RIM - 1), (3 * RIM - 1, 2 * RIM))


def rim_kernel(taps_ref, a_ref, b_ref, out_ref):
    odd = lax.axis_index("tx") % 2 > 0
    cols = out_ref.shape[1]
    taps = taps_ref[...]
    taps = jnp.concatenate([taps, jnp.zeros((1, cols - taps.shape[1]), jnp.float32)], 1)
    hi = taps.astype(jnp.bfloat16).astype(jnp.float32)
    mid = (taps - hi).astype(jnp.bfloat16).astype(jnp.float32)
    rims = jnp.concatenate([a_ref[...].astype(jnp.float32), b_ref[...].astype(jnp.float32)], 0)
    row = lax.broadcasted_iota(jnp.int32, rims.shape, 0)
    for (on_odd, on_even), part in zip(SPARE, (hi, mid, taps - hi - mid)):
        rims = jnp.where(row == jnp.where(odd, on_odd, on_even), part, rims)
    out_ref[...] = rims.astype(jnp.bfloat16)


def turned(pieces, by):
    count = len(pieces)
    whole, part = divmod(by, 128)
    near = pieces[-whole % count]
    if part == 0:
        return near
    far = pieces[(-whole - 1) % count]
    lane = lax.broadcasted_iota(jnp.int32, near.shape, 1)
    return jnp.where(lane >= part, pltpu.roll(near, part, 1), pltpu.roll(far, part, 1))


def cut(base):
    return [base[:, j : j + 128] for j in range(0, base.shape[1], 128)]


def select(d, weights):
    acc = jnp.zeros(d.shape, jnp.float32)
    for a, w in enumerate(weights):
        acc = jnp.where(d == a, w, acc)
    return acc.astype(jnp.bfloat16)


def distance(count, source_axis):
    d = lax.broadcasted_iota(jnp.int32, (16, count), source_axis) - lax.broadcasted_iota(
        jnp.int32, (16, count), 1 - source_axis
    )
    return d


def shift_kernel(hyps, rows, all_cols, base_ref, times_ref, speed_ref, rb_ref, cb_ref):
    circle = rb_ref.shape[2]
    row_base = distance(circle, 1)
    col_base = distance(all_cols, 0)

    def one(e, carry):
        time = times_ref[lax.axis_index("ea") ^ (base_ref[0] + e)]
        for h in range(hyps):
            whole, weights = spline_taps(speed_ref[h, 0], time)
            pieces = cut(select((row_base - (whole - 1)) & (circle - 1), weights))
            turns = [pieces[-j:] + pieces[:-j] for j in range(len(pieces), 0, -1)]
            for n in range(0, rows, 16):
                for j, turn in enumerate(turns):
                    rb_ref[e, h * rows + n : h * rows + n + 16, 128 * j : 128 * (j + 1)] = turned(turn, n)
            whole, weights = spline_taps(speed_ref[h, 1], time)
            d = col_base - (whole - 1)
            pieces = cut(select(jnp.where(d < 0, d + all_cols, d), weights))
            for n in range(0, all_cols, 16):
                cb_ref[h, e, n : n + 16, :] = turned(pieces, n)
        return carry

    lax.fori_loop(0, rb_ref.shape[0], one, 0)


def held_taps(halo_ref):
    odd = lax.axis_index("tx") % 2 > 0

    def held(row):
        block = halo_ref[row // 16 * 16 : row // 16 * 16 + 16, :].astype(jnp.float32)
        return block[row % 16 : row % 16 + 1]

    return sum(jnp.where(odd, held(on_odd), held(on_even)) for on_odd, on_even in SPARE)


def blur_kernel(rows, cols, last_x, *refs):
    count = len(refs) // 5
    tiles, halos, outs = refs[:count], refs[count : 2 * count], refs[2 * count :]
    for j in range(count):
        br, bc, half = outs[3 * j : 3 * j + 3]
        blur_bands(rows, cols, last_x, held_taps(halos[j]), br, bc)
        for i in range(2):
            half[i] = row_blur(rows, i, tiles[j], halos[j], br)


def row_blur(rows, i, tile, halo, br):
    field = [tile[i * rows : (i + 1) * rows, :], halo[16 * i : 16 * i + 128, :]]
    return dot(br[i], jnp.concatenate(field, 0)).astype(jnp.bfloat16)


def blur_bands(rows, cols, last_x, p, br_ref, bc_ref):
    out_rows, circle = br_ref.shape[1:]
    all_cols = bc_ref.shape[1]
    here_x = lax.axis_index("tx")
    odd = here_x % 2 > 0
    one = jnp.ones((16, 128), jnp.float32)
    keep_above = jnp.where(here_x > 0, one, 0.0).astype(jnp.bfloat16)
    keep_below = jnp.where(here_x < last_x, one, 0.0).astype(jnp.bfloat16)
    p = p / jnp.sum(p, axis=1, keepdims=True)
    taps = [p[:, t : t + 1] for t in range(2 * PR + 1)]
    kernels = (taps, [t * t for t in taps])
    row_base = (distance(circle, 1) + PR) & (circle - 1)
    col_base = distance(all_cols, 0) + PR
    col_base = jnp.where(col_base < 0, col_base + all_cols, col_base)
    lane = lax.broadcasted_iota(jnp.int32, (16, 128), 1)
    for i in range(2):
        pieces = cut(select(row_base, kernels[i]))
        first_a = (RIM - 16) * i
        first_b = 2 * RIM + first_a

        def rim(n, lanes, coordinate):
            return jnp.where(
                (lane >= lanes) & (lane < lanes + RIM), turned(pieces, (n + lanes - coordinate) % circle), 0.0
            ).astype(jnp.bfloat16)

        for at in range(0, out_rows, 16):
            n = at if at < rows + REACH else at - out_rows
            left = turned(pieces, n % circle)
            right = jnp.zeros((16, 128), jnp.bfloat16)
            if n - PR < 0:
                right = jnp.where(odd, rim(n, first_a, -RIM), rim(n, first_b, -RIM))
            elif n + 16 + PR > rows:
                right = jnp.where(odd, rim(n, first_b, rows), rim(n, first_a, rows))
            if n < 0 or n >= rows:
                keep = keep_above if n < 0 else keep_below
                left, right = left * keep, right * keep
            br_ref[i, at : at + 16, :128] = left
            br_ref[i, at : at + 16, 128:] = right
        pieces = cut(select(col_base, kernels[i]))
        for n in range(0, all_cols, 16):
            bc_ref[i, n : n + 16, :] = turned(pieces, n)


def dot(a, b):
    return jnp.dot(a, b, preferred_element_type=jnp.float32)


def widen(c, count):
    total = c.shape[0]
    return jnp.concatenate(
        [c] + [jnp.concatenate([c[total - 128 * j :], c[: total - 128 * j]], 0) for j in range(1, count)],
        1,
    )


def stack_kernel(slots, hyps, rows, cols, last_y, first, final, spots, *refs):
    count = len(slots)
    refs = list(refs)
    made, brs, bcs = [[refs.pop(0) for _ in range(count)] for _ in range(3)]
    side_tiles, side_halos, rb, cb = [refs.pop(0) for _ in range(4)]
    acc = None if first else refs.pop(0)
    out = refs.pop(0)
    wide = cols + 128
    lane = lax.broadcasted_iota(jnp.int32, (1, 128), 1)
    here_y = lax.axis_index("ty")
    after = jnp.where((lane < 64) & (here_y < last_y), 1.0, 0.0)
    before = jnp.where((lane >= 64) & (here_y > 0), 1.0, 0.0)
    side = (after + before).astype(jnp.bfloat16)
    after = after.astype(jnp.bfloat16)
    before = before.astype(jnp.bfloat16)
    upper = rows + REACH
    unused = jnp.zeros((rb.shape[2] - rows - 2 * REACH, wide), jnp.float32)
    moved = []
    for j in range(count):
        pair = []
        tile_at, halo_at = spots[j]
        for i in range(2):
            at = i * rows
            rim = 16 * i
            right = [
                side_tiles[tile_at + at : tile_at + at + rows, :],
                side_halos[halo_at + rim : halo_at + rim + 128, :],
            ]
            right = jnp.concatenate(right, 0)
            right = right[:, :128] * after + right[:, cols - 128 :] * before
            half = jnp.concatenate([made[j][i], dot(brs[j][i], right).astype(jnp.bfloat16)], 1)
            image = dot(half, widen(bcs[j][i], wide // 128))
            image = jnp.concatenate([image[:upper], unused, image[upper:]], 0).astype(jnp.bfloat16)
            pair += [image[:, :cols], image[:, cols:] * side]
        moved.append(dot(rb[slots[j]], jnp.concatenate(pair, 1)).astype(jnp.bfloat16))
    copies = []
    for h in range(hyps):
        at = slice(h * rows, (h + 1) * rows)
        both = [jnp.concatenate([m[at, :wide], m[at, wide:]], 0) for m in moved]
        bands = [widen(cb[h, k], cols // 128) for k in slots]
        total = dot(jnp.concatenate(both, 1), jnp.concatenate(bands, 0))
        if not first:
            total = total + acc[h]
        if final:
            held, sems = refs
            held[h] = total[:rows] * lax.rsqrt(total[rows:])
            copies.append(pltpu.make_async_copy(held.at[h], out.at[h], sems.at[h]))
            copies[-1].start()
        else:
            out[h] = total
    for copy in copies:
        copy.wait()


VMEM = pl.BlockSpec(memory_space=pltpu.VMEM)
SMEM = pl.BlockSpec(memory_space=pltpu.SMEM)
PARAMS = pltpu.CompilerParams(vmem_limit_bytes=VMEM_LIMIT)


def call(kernel, specs, shapes, *args, scratch=(), flops=0, out=VMEM):
    single = not isinstance(shapes, (list, tuple))
    return pl.pallas_call(
        kernel,
        out_shape=shapes,
        in_specs=specs,
        out_specs=out if single else [out] * len(shapes),
        scratch_shapes=list(scratch),
        compiler_params=PARAMS,
        cost_estimate=pl.CostEstimate(flops=flops, bytes_accessed=0, transcendentals=0),
    )(*args)


def bf16(*shape):
    return jax.ShapeDtypeStruct(shape, jnp.bfloat16)


def side_swap(x):
    count = lax.axis_size("ty")
    if count == 2:
        return lax.ppermute(x, "ty", [(0, 1), (1, 0)])
    after = lax.ppermute(x[:, :128], "ty", [(i + 1, i) for i in range(count - 1)])
    before = lax.ppermute(x[:, x.shape[1] - 128 :], "ty", [(i, i + 1) for i in range(count - 1)])
    return jnp.concatenate([after, before], 1)


def shards(science, inv_variance, psf_taps, epoch_times, velocities):
    rows, cols = science.shape[1:]
    hyps = velocities.shape[0]
    epochs = lax.axis_size("ea")
    tx = lax.axis_size("tx")
    ty = lax.axis_size("ty")
    all_cols = cols + 128
    slots = min(GROUP, epochs)

    own = jnp.concatenate([science[0] * inv_variance[0], inv_variance[0]], 0).astype(jnp.bfloat16)
    tiles = [own] + [
        lax.ppermute(own, "ea", [(i, i ^ k) for i in range(epochs)]) for k in range(1, epochs)
    ]
    cut_from = own
    if epochs == slots:
        pass
    strip_a, strip_b = call(
        functools.partial(strip_kernel, rows),
        [VMEM],
        [bf16(2 * RIM, cols)] * 2,
        cut_from,
        flops=STRIP_FLOPS,
    )
    swap_b = [(i, i + 1) for i in range(1, tx - 1, 2)] + [(i + 1, i) for i in range(1, tx - 1, 2)]
    swap_a = [(i, i + 1) for i in range(0, tx - 1, 2)] + [(i + 1, i) for i in range(0, tx - 1, 2)]
    rim_b = lax.ppermute(strip_b, "tx", swap_b)
    rim_a = lax.ppermute(strip_a, "tx", swap_a)
    halo = call(rim_kernel, [VMEM] * 3, bf16(4 * RIM, cols), psf_taps, rim_a, rim_b, flops=STRIP_FLOPS)
    band_shapes = [bf16(2, rows + 2 * REACH, 2 * rows), bf16(2, all_cols, 128)]

    def shift_bands(base):
        return call(
            functools.partial(shift_kernel, hyps, rows, all_cols),
            [SMEM] * 3,
            [bf16(slots, hyps * rows, 2 * rows), bf16(hyps, slots, all_cols, 128)],
            base,
            epoch_times,
            velocities,
            flops=SHIFT_FLOPS,
        )

    def blurred(tiles, halos):
        count = len(halos)
        made = call(
            functools.partial(blur_kernel, rows, cols, tx - 1),
            [VMEM] * (2 * count),
            [*band_shapes, bf16(2, rows + 2 * REACH, cols)] * count,
            *tiles,
            *halos,
            flops=BLUR_FLOPS,
        )
        return [made[j::3] for j in range(3)]

    def stack(slots, made, brs, bcs, side_tiles, side_halos, shifts, total, final):
        args = [*made, *brs, *bcs, side_tiles, side_halos, *shifts]
        if total is not None:
            args.append(total)
        shape = (hyps, rows, cols) if final else (hyps, 2 * rows, cols)
        shape = jax.ShapeDtypeStruct(shape, jnp.float32)
        spots = [(j * own.shape[0], j * halo.shape[0]) for j in range(len(slots))]
        return call(
            functools.partial(
                stack_kernel, slots, hyps, rows, cols, ty - 1, total is None, final, spots
            ),
            [VMEM] * len(args),
            shape,
            *args,
            flops=STACK_FLOPS,
            out=pl.BlockSpec(memory_space=pltpu.HBM) if final else VMEM,
            scratch=[pltpu.VMEM(shape.shape, jnp.float32), pltpu.SemaphoreType.DMA((hyps,))] if final else [],
        )

    def beside(arrays):
        return side_swap(jnp.concatenate(arrays, 0))

    if epochs == slots:
        shifts = shift_bands(jnp.zeros((1,), jnp.int32))
        *shifts, halo = lax.optimization_barrier((*shifts, halo))
        halos = [halo] + [
            lax.ppermute(halo, "ea", [(i, i ^ k) for i in range(epochs)]) for k in range(1, epochs)
        ]
        side = beside([own, halo])
        brs, bcs, made = blurred([own], [halo])
        total = stack([0], made, brs, bcs, side[: own.shape[0]], side[own.shape[0] :], shifts, None, False)
        taken = [3, 1, 2]
        others = lax.optimization_barrier([tiles[k] for k in taken])
        others = [others[taken.index(k)] for k in range(1, epochs)]
        later = beside(others)
        taken = [1, 3, 2]
        total, later, *rest = lax.optimization_barrier((total, later, *[halos[k] for k in taken]))
        rims = [rest[taken.index(k)] for k in range(1, epochs)]
        brs, bcs, made = blurred(others, rims)
        return stack(list(range(1, epochs)), made, brs, bcs, later, beside(rims), shifts, total, True)

    halos = [halo] + [
        lax.ppermute(halo, "ea", [(i, i ^ k) for i in range(epochs)]) for k in range(1, epochs)
    ]

    def step(total, xs):
        tiles, halos, base = xs
        tiles = [tiles[k] for k in range(slots)]
        halos = [halos[k] for k in range(slots)]
        brs, bcs, made = blurred(tiles, halos)
        sides = beside(tiles), beside(halos)
        return stack(list(range(slots)), made, brs, bcs, *sides, shift_bands(base), total, False), None

    split = lambda x: x.reshape((epochs // slots, slots) + x.shape[1:])
    zeros = jnp.zeros((hyps, 2 * rows, cols), jnp.float32)
    bases = jnp.arange(0, epochs, slots, dtype=jnp.int32)[:, None]
    every = (split(jnp.stack(tiles)), split(jnp.stack(halos)), bases)
    total, _ = lax.scan(step, zeros, every)
    return total[:, :rows] / jnp.sqrt(total[:, rows:])


def solution(mesh):
    in_specs = (P("ea", "tx", "ty"), P("ea", "tx", "ty"), P("ea", None), P(), P("ea", None))
    out_specs = P("ea", "tx", "ty")
    return jax.shard_map(shards, mesh=mesh, in_specs=in_specs, out_specs=out_specs, check_vma=False)
```

```python
import functools

import jax
import jax.numpy as jnp
from jax import lax
from jax.experimental import pallas as pl
from jax.experimental.pallas import tpu as pltpu
from jax.sharding import PartitionSpec as P

REACH = 32
PR = 4
RIM = REACH + PR
GROUP = 4
VMEM_LIMIT = 24 * 1024 * 1024
STRIP_FLOPS = 10_000_000
SHIFT_FLOPS = 4_000_000_000
BLUR_FLOPS = 4_000_000_000
STACK_FLOPS = 2_000_000_000


def spline_taps(speed, time):
    moved = (speed * time) >> 3
    frac = (moved & 15).astype(jnp.float32) * (1.0 / 16.0)
    rest = 1.0 - frac
    frac2 = frac * frac
    frac3 = frac2 * frac
    sixth = 1.0 / 6.0
    weights = [
        rest * rest * rest * sixth,
        (3.0 * frac3 - 6.0 * frac2 + 4.0) * sixth,
        (-3.0 * frac3 + 3.0 * frac2 + 3.0 * frac + 1.0) * sixth,
        frac3 * sixth,
    ]
    return moved >> 4, weights


def strip_kernel(rows, own_ref, a_ref, b_ref):
    odd = lax.axis_index("tx") % 2 > 0
    heads, tails = [], []
    for i in range(2):
        x = own_ref[i * rows : (i + 1) * rows, :].astype(jnp.float32)
        heads.append(x[:RIM])
        tails.append(x[rows - RIM :])
    head = jnp.concatenate(heads, 0)
    tail = jnp.concatenate(tails, 0)
    a_ref[...] = jnp.where(odd, head, tail).astype(jnp.bfloat16)
    b_ref[...] = jnp.where(odd, tail, head).astype(jnp.bfloat16)


SPARE = ((0, RIM - 1), (RIM, 2 * RIM - 1), (3 * RIM - 1, 2 * RIM))


def rim_kernel(taps_ref, a_ref, b_ref, out_ref):
    odd = lax.axis_index("tx") % 2 > 0
    cols = out_ref.shape[1]
    taps = taps_ref[...]
    taps = jnp.concatenate([taps, jnp.zeros((1, cols - taps.shape[1]), jnp.float32)], 1)
    hi = taps.astype(jnp.bfloat16).astype(jnp.float32)
    mid = (taps - hi).astype(jnp.bfloat16).astype(jnp.float32)
    rims = jnp.concatenate([a_ref[...].astype(jnp.float32), b_ref[...].astype(jnp.float32)], 0)
    row = lax.broadcasted_iota(jnp.int32, rims.shape, 0)
    for (on_odd, on_even), part in zip(SPARE, (hi, mid, taps - hi - mid)):
        rims = jnp.where(row == jnp.where(odd, on_odd, on_even), part, rims)
    out_ref[...] = rims.astype(jnp.bfloat16)


def turned(pieces, by):
    count = len(pieces)
    whole, part = divmod(by, 128)
    near = pieces[-whole % count]
    if part == 0:
        return near
    far = pieces[(-whole - 1) % count]
    lane = lax.broadcasted_iota(jnp.int32, near.shape, 1)
    return jnp.where(lane >= part, pltpu.roll(near, part, 1), pltpu.roll(far, part, 1))


def cut(base):
    return [base[:, j : j + 128] for j in range(0, base.shape[1], 128)]


def select(d, weights):
    acc = jnp.zeros(d.shape, jnp.float32)
    for a, w in enumerate(weights):
        acc = jnp.where(d == a, w, acc)
    return acc.astype(jnp.bfloat16)


def distance(count, source_axis):
    d = lax.broadcasted_iota(jnp.int32, (16, count), source_axis) - lax.broadcasted_iota(
        jnp.int32, (16, count), 1 - source_axis
    )
    return d


def shift_kernel(hyps, rows, all_cols, base_ref, times_ref, speed_ref, rb_ref, cb_ref):
    circle = rb_ref.shape[2]
    row_base = distance(circle, 1)
    col_base = distance(all_cols, 0)

    def one(e, carry):
        time = times_ref[lax.axis_index("ea") ^ (base_ref[0] + e)]
        for h in range(hyps):
            whole, weights = spline_taps(speed_ref[h, 0], time)
            pieces = cut(select((row_base - (whole - 1)) & (circle - 1), weights))
            turns = [pieces[-j:] + pieces[:-j] for j in range(len(pieces), 0, -1)]
            for n in range(0, rows, 16):
                for j, turn in enumerate(turns):
                    rb_ref[e, h * rows + n : h * rows + n + 16, 128 * j : 128 * (j + 1)] = turned(turn, n)
            whole, weights = spline_taps(speed_ref[h, 1], time)
            d = col_base - (whole - 1)
            pieces = cut(select(jnp.where(d < 0, d + all_cols, d), weights))
            for n in range(0, all_cols, 16):
                cb_ref[h, e, n : n + 16, :] = turned(pieces, n)
        return carry

    lax.fori_loop(0, rb_ref.shape[0], one, 0)


def held_taps(halo_ref):
    odd = lax.axis_index("tx") % 2 > 0

    def held(row):
        block = halo_ref[row // 16 * 16 : row // 16 * 16 + 16, :].astype(jnp.float32)
        return block[row % 16 : row % 16 + 1]

    return sum(jnp.where(odd, held(on_odd), held(on_even)) for on_odd, on_even in SPARE)


def blur_kernel(rows, cols, last_x, *refs):
    count = len(refs) // 6
    tiles, halos, outs = refs[:count], refs[count : 2 * count], refs[2 * count :]
    for j in range(count):
        br, bc, scale, half = outs[4 * j : 4 * j + 4]
        blur_bands(rows, cols, last_x, held_taps(halos[j]), br, bc, scale)
        for i in range(2):
            half[i] = row_blur(rows, i, tiles[j], halos[j], br)


def row_blur(rows, i, tile, halo, br):
    field = [tile[i * rows : (i + 1) * rows, :], halo[16 * i : 16 * i + 128, :]]
    return dot(br[i], jnp.concatenate(field, 0)).astype(jnp.bfloat16)


def blur_bands(rows, cols, last_x, p, br_ref, bc_ref, scale_ref):
    out_rows, circle = br_ref.shape[1:]
    all_cols = bc_ref.shape[1]
    here_x = lax.axis_index("tx")
    odd = here_x % 2 > 0
    one = jnp.ones((16, 128), jnp.float32)
    keep_above = jnp.where(here_x > 0, one, 0.0).astype(jnp.bfloat16)
    keep_below = jnp.where(here_x < last_x, one, 0.0).astype(jnp.bfloat16)
    p = p / jnp.sum(p, axis=1, keepdims=True)
    taps = [p[:, t : t + 1] for t in range(2 * PR + 1)]
    kernels = (taps, [t * t for t in taps])
    row_base = (distance(circle, 1) + PR) & (circle - 1)
    col_base = distance(all_cols, 0) + PR
    col_base = jnp.where(col_base < 0, col_base + all_cols, col_base)
    lane = lax.broadcasted_iota(jnp.int32, (16, 128), 1)
    for i in range(2):
        rounded = sum(t.astype(jnp.bfloat16).astype(jnp.float32) for t in kernels[i])
        ratio = sum(kernels[i]) / rounded
        scale_ref[i] = jnp.broadcast_to(ratio * ratio, scale_ref.shape[1:])
        pieces = cut(select(row_base, kernels[i]))
        first_a = (RIM - 16) * i
        first_b = 2 * RIM + first_a

        def rim(n, lanes, coordinate):
            return jnp.where(
                (lane >= lanes) & (lane < lanes + RIM), turned(pieces, (n + lanes - coordinate) % circle), 0.0
            ).astype(jnp.bfloat16)

        for at in range(0, out_rows, 16):
            n = at if at < rows + REACH else at - out_rows
            left = turned(pieces, n % circle)
            right = jnp.zeros((16, 128), jnp.bfloat16)
            if n - PR < 0:
                right = jnp.where(odd, rim(n, first_a, -RIM), rim(n, first_b, -RIM))
            elif n + 16 + PR > rows:
                right = jnp.where(odd, rim(n, first_b, rows), rim(n, first_a, rows))
            if n < 0 or n >= rows:
                keep = keep_above if n < 0 else keep_below
                left, right = left * keep, right * keep
            br_ref[i, at : at + 16, :128] = left
            br_ref[i, at : at + 16, 128:] = right
        pieces = cut(select(col_base, kernels[i]))
        for n in range(0, all_cols, 16):
            bc_ref[i, n : n + 16, :] = turned(pieces, n)


def dot(a, b):
    return jnp.dot(a, b, preferred_element_type=jnp.float32)


def widen(c, count):
    total = c.shape[0]
    return jnp.concatenate(
        [c] + [jnp.concatenate([c[total - 128 * j :], c[: total - 128 * j]], 0) for j in range(1, count)],
        1,
    )


def stack_kernel(slots, hyps, rows, cols, last_y, first, final, spots, *refs):
    count = len(slots)
    refs = list(refs)
    made, brs, bcs, scales = [[refs.pop(0) for _ in range(count)] for _ in range(4)]
    side_tiles, side_halos, rb, cb = [refs.pop(0) for _ in range(4)]
    acc = None if first else refs.pop(0)
    out = refs.pop(0)
    wide = cols + 128
    lane = lax.broadcasted_iota(jnp.int32, (1, 128), 1)
    here_y = lax.axis_index("ty")
    after = jnp.where((lane < 64) & (here_y < last_y), 1.0, 0.0)
    before = jnp.where((lane >= 64) & (here_y > 0), 1.0, 0.0)
    side = (after + before).astype(jnp.bfloat16)
    after = after.astype(jnp.bfloat16)
    before = before.astype(jnp.bfloat16)
    upper = rows + REACH
    unused = jnp.zeros((rb.shape[2] - rows - 2 * REACH, wide), jnp.float32)
    moved = []
    for j in range(count):
        pair = []
        tile_at, halo_at = spots[j]
        for i in range(2):
            at = i * rows
            rim = 16 * i
            right = [
                side_tiles[tile_at + at : tile_at + at + rows, :],
                side_halos[halo_at + rim : halo_at + rim + 128, :],
            ]
            right = jnp.concatenate(right, 0)
            right = right[:, :128] * after + right[:, cols - 128 :] * before
            half = jnp.concatenate([made[j][i], dot(brs[j][i], right).astype(jnp.bfloat16)], 1)
            image = dot(half, widen(bcs[j][i], wide // 128)) * scales[j][i, 0:1, :]
            image = jnp.concatenate([image[:upper], unused, image[upper:]], 0).astype(jnp.bfloat16)
            pair += [image[:, :cols], image[:, cols:] * side]
        moved.append(dot(rb[slots[j]], jnp.concatenate(pair, 1)).astype(jnp.bfloat16))
    copies = []
    for h in range(hyps):
        at = slice(h * rows, (h + 1) * rows)
        both = [jnp.concatenate([m[at, :wide], m[at, wide:]], 0) for m in moved]
        bands = [widen(cb[h, k], cols // 128) for k in slots]
        total = dot(jnp.concatenate(both, 1), jnp.concatenate(bands, 0))
        if not first:
            total = total + acc[h]
        if final:
            held, sems = refs
            held[h] = total[:rows] * lax.rsqrt(total[rows:])
            copies.append(pltpu.make_async_copy(held.at[h], out.at[h], sems.at[h]))
            copies[-1].start()
        else:
            out[h] = total
    for copy in copies:
        copy.wait()


VMEM = pl.BlockSpec(memory_space=pltpu.VMEM)
SMEM = pl.BlockSpec(memory_space=pltpu.SMEM)
PARAMS = pltpu.CompilerParams(vmem_limit_bytes=VMEM_LIMIT)


def call(kernel, specs, shapes, *args, scratch=(), flops=0, out=VMEM):
    single = not isinstance(shapes, (list, tuple))
    return pl.pallas_call(
        kernel,
        out_shape=shapes,
        in_specs=specs,
        out_specs=out if single else [out] * len(shapes),
        scratch_shapes=list(scratch),
        compiler_params=PARAMS,
        cost_estimate=pl.CostEstimate(flops=flops, bytes_accessed=0, transcendentals=0),
    )(*args)


def bf16(*shape):
    return jax.ShapeDtypeStruct(shape, jnp.bfloat16)


def side_swap(x):
    count = lax.axis_size("ty")
    if count == 2:
        return lax.ppermute(x, "ty", [(0, 1), (1, 0)])
    after = lax.ppermute(x[:, :128], "ty", [(i + 1, i) for i in range(count - 1)])
    before = lax.ppermute(x[:, x.shape[1] - 128 :], "ty", [(i, i + 1) for i in range(count - 1)])
    return jnp.concatenate([after, before], 1)


def shards(science, inv_variance, psf_taps, epoch_times, velocities):
    rows, cols = science.shape[1:]
    hyps = velocities.shape[0]
    epochs = lax.axis_size("ea")
    tx = lax.axis_size("tx")
    ty = lax.axis_size("ty")
    all_cols = cols + 128
    slots = min(GROUP, epochs)

    own = jnp.concatenate([science[0] * inv_variance[0], inv_variance[0]], 0).astype(jnp.bfloat16)
    tiles = [own] + [
        lax.ppermute(own, "ea", [(i, i ^ k) for i in range(epochs)]) for k in range(1, epochs)
    ]
    cut_from = own
    if epochs == slots:
        pass
    strip_a, strip_b = call(
        functools.partial(strip_kernel, rows),
        [VMEM],
        [bf16(2 * RIM, cols)] * 2,
        cut_from,
        flops=STRIP_FLOPS,
    )
    swap_b = [(i, i + 1) for i in range(1, tx - 1, 2)] + [(i + 1, i) for i in range(1, tx - 1, 2)]
    swap_a = [(i, i + 1) for i in range(0, tx - 1, 2)] + [(i + 1, i) for i in range(0, tx - 1, 2)]
    rim_b = lax.ppermute(strip_b, "tx", swap_b)
    rim_a = lax.ppermute(strip_a, "tx", swap_a)
    halo = call(rim_kernel, [VMEM] * 3, bf16(4 * RIM, cols), psf_taps, rim_a, rim_b, flops=STRIP_FLOPS)
    band_shapes = [
        bf16(2, rows + 2 * REACH, 2 * rows),
        bf16(2, all_cols, 128),
        jax.ShapeDtypeStruct((2, 8, all_cols), jnp.float32),
    ]

    def shift_bands(base):
        return call(
            functools.partial(shift_kernel, hyps, rows, all_cols),
            [SMEM] * 3,
            [bf16(slots, hyps * rows, 2 * rows), bf16(hyps, slots, all_cols, 128)],
            base,
            epoch_times,
            velocities,
            flops=SHIFT_FLOPS,
        )

    def blurred(tiles, halos):
        count = len(halos)
        made = call(
            functools.partial(blur_kernel, rows, cols, tx - 1),
            [VMEM] * (2 * count),
            [*band_shapes, bf16(2, rows + 2 * REACH, cols)] * count,
            *tiles,
            *halos,
            flops=BLUR_FLOPS,
        )
        return [made[j::4] for j in range(4)]

    def stack(slots, made, blurs, side_tiles, side_halos, shifts, total, final):
        args = [*made, *[x for kind in blurs for x in kind], side_tiles, side_halos, *shifts]
        if total is not None:
            args.append(total)
        shape = (hyps, rows, cols) if final else (hyps, 2 * rows, cols)
        shape = jax.ShapeDtypeStruct(shape, jnp.float32)
        spots = [(j * own.shape[0], j * halo.shape[0]) for j in range(len(slots))]
        return call(
            functools.partial(
                stack_kernel, slots, hyps, rows, cols, ty - 1, total is None, final, spots
            ),
            [VMEM] * len(args),
            shape,
            *args,
            flops=STACK_FLOPS,
            out=pl.BlockSpec(memory_space=pltpu.HBM) if final else VMEM,
            scratch=[pltpu.VMEM(shape.shape, jnp.float32), pltpu.SemaphoreType.DMA((hyps,))] if final else [],
        )

    def beside(arrays):
        return side_swap(jnp.concatenate(arrays, 0))

    if epochs == slots:
        shifts = shift_bands(jnp.zeros((1,), jnp.int32))
        *shifts, halo = lax.optimization_barrier((*shifts, halo))
        halos = [halo] + [
            lax.ppermute(halo, "ea", [(i, i ^ k) for i in range(epochs)]) for k in range(1, epochs)
        ]
        side = beside([own, halo])
        *blurs, made = blurred([own], [halo])
        total = stack([0], made, blurs, side[: own.shape[0]], side[own.shape[0] :], shifts, None, False)
        taken = [3, 1, 2]
        others = lax.optimization_barrier([tiles[k] for k in taken])
        others = [others[taken.index(k)] for k in range(1, epochs)]
        later = beside(others)
        taken = [1, 3, 2]
        total, later, *rest = lax.optimization_barrier((total, later, *[halos[k] for k in taken]))
        rims = [rest[taken.index(k)] for k in range(1, epochs)]
        *blurs, made = blurred(others, rims)
        return stack(list(range(1, epochs)), made, blurs, later, beside(rims), shifts, total, True)

    halos = [halo] + [
        lax.ppermute(halo, "ea", [(i, i ^ k) for i in range(epochs)]) for k in range(1, epochs)
    ]

    def step(total, xs):
        tiles, halos, base = xs
        tiles = [tiles[k] for k in range(slots)]
        halos = [halos[k] for k in range(slots)]
        *blurs, made = blurred(tiles, halos)
        sides = beside(tiles), beside(halos)
        return stack(list(range(slots)), made, blurs, *sides, shift_bands(base), total, False), None

    split = lambda x: x.reshape((epochs // slots, slots) + x.shape[1:])
    zeros = jnp.zeros((hyps, 2 * rows, cols), jnp.float32)
    bases = jnp.arange(0, epochs, slots, dtype=jnp.int32)[:, None]
    every = (split(jnp.stack(tiles)), split(jnp.stack(halos)), bases)
    total, _ = lax.scan(step, zeros, every)
    return total[:, :rows] / jnp.sqrt(total[:, rows:])


def solution(mesh):
    in_specs = (P("ea", "tx", "ty"), P("ea", "tx", "ty"), P("ea", None), P(), P("ea", None))
    out_specs = P("ea", "tx", "ty")
    return jax.shard_map(shards, mesh=mesh, in_specs=in_specs, out_specs=out_specs, check_vma=False)
```

```python
import functools

import jax
import jax.numpy as jnp
from jax import lax
from jax.experimental import pallas as pl
from jax.experimental.pallas import tpu as pltpu
from jax.sharding import PartitionSpec as P

REACH = 32
PR = 4
RIM = REACH + PR
GROUP = 4
VMEM_LIMIT = 24 * 1024 * 1024
STRIP_FLOPS = 4_000_000_000
SHIFT_FLOPS = 4_000_000_000
BLUR_FLOPS = 4_000_000_000
STACK_FLOPS = 2_000_000_000


def spline_taps(speed, time):
    moved = (speed * time) >> 3
    frac = (moved & 15).astype(jnp.float32) * (1.0 / 16.0)
    rest = 1.0 - frac
    frac2 = frac * frac
    frac3 = frac2 * frac
    sixth = 1.0 / 6.0
    weights = [
        rest * rest * rest * sixth,
        (3.0 * frac3 - 6.0 * frac2 + 4.0) * sixth,
        (-3.0 * frac3 + 3.0 * frac2 + 3.0 * frac + 1.0) * sixth,
        frac3 * sixth,
    ]
    return moved >> 4, weights


def strip_kernel(rows, own_ref, a_ref, b_ref):
    odd = lax.axis_index("tx") % 2 > 0
    heads, tails = [], []
    for i in range(2):
        x = own_ref[i * rows : (i + 1) * rows, :].astype(jnp.float32)
        heads.append(x[:RIM])
        tails.append(x[rows - RIM :])
    head = jnp.concatenate(heads, 0)
    tail = jnp.concatenate(tails, 0)
    a_ref[...] = jnp.where(odd, head, tail).astype(jnp.bfloat16)
    b_ref[...] = jnp.where(odd, tail, head).astype(jnp.bfloat16)


SPARE = ((0, RIM - 1), (RIM, 2 * RIM - 1), (3 * RIM - 1, 2 * RIM))


def rim_kernel(taps_ref, a_ref, b_ref, out_ref):
    odd = lax.axis_index("tx") % 2 > 0
    cols = out_ref.shape[1]
    taps = taps_ref[...]
    taps = jnp.concatenate([taps, jnp.zeros((1, cols - taps.shape[1]), jnp.float32)], 1)
    hi = taps.astype(jnp.bfloat16).astype(jnp.float32)
    mid = (taps - hi).astype(jnp.bfloat16).astype(jnp.float32)
    rims = jnp.concatenate([a_ref[...].astype(jnp.float32), b_ref[...].astype(jnp.float32)], 0)
    row = lax.broadcasted_iota(jnp.int32, rims.shape, 0)
    for (on_odd, on_even), part in zip(SPARE, (hi, mid, taps - hi - mid)):
        rims = jnp.where(row == jnp.where(odd, on_odd, on_even), part, rims)
    out_ref[...] = rims.astype(jnp.bfloat16)


def turned(pieces, by):
    count = len(pieces)
    whole, part = divmod(by, 128)
    near = pieces[-whole % count]
    if part == 0:
        return near
    far = pieces[(-whole - 1) % count]
    lane = lax.broadcasted_iota(jnp.int32, near.shape, 1)
    return jnp.where(lane >= part, pltpu.roll(near, part, 1), pltpu.roll(far, part, 1))


def cut(base):
    return [base[:, j : j + 128] for j in range(0, base.shape[1], 128)]


def select(d, weights):
    acc = jnp.zeros(d.shape, jnp.float32)
    for a, w in enumerate(weights):
        acc = jnp.where(d == a, w, acc)
    return acc.astype(jnp.bfloat16)


def distance(count, source_axis):
    d = lax.broadcasted_iota(jnp.int32, (16, count), source_axis) - lax.broadcasted_iota(
        jnp.int32, (16, count), 1 - source_axis
    )
    return d


def shift_kernel(hyps, rows, all_cols, base_ref, times_ref, speed_ref, rb_ref, cb_ref):
    circle = rb_ref.shape[2]
    row_base = distance(circle, 1)
    col_base = distance(all_cols, 0)

    def one(e, carry):
        time = times_ref[lax.axis_index("ea") ^ (base_ref[0] + e)]
        for h in range(hyps):
            whole, weights = spline_taps(speed_ref[h, 0], time)
            pieces = cut(select((row_base - (whole - 1)) & (circle - 1), weights))
            turns = [pieces[-j:] + pieces[:-j] for j in range(len(pieces), 0, -1)]
            for n in range(0, rows, 16):
                for j, turn in enumerate(turns):
                    rb_ref[e, h * rows + n : h * rows + n + 16, 128 * j : 128 * (j + 1)] = turned(turn, n)
            whole, weights = spline_taps(speed_ref[h, 1], time)
            d = col_base - (whole - 1)
            pieces = cut(select(jnp.where(d < 0, d + all_cols, d), weights))
            for n in range(0, all_cols, 16):
                cb_ref[h, e, n : n + 16, :] = turned(pieces, n)
        return carry

    lax.fori_loop(0, rb_ref.shape[0], one, 0)


def held_taps(halo_ref):
    odd = lax.axis_index("tx") % 2 > 0

    def held(row):
        block = halo_ref[row // 16 * 16 : row // 16 * 16 + 16, :].astype(jnp.float32)
        return block[row % 16 : row % 16 + 1]

    return sum(jnp.where(odd, held(on_odd), held(on_even)) for on_odd, on_even in SPARE)


def blur_kernel(rows, cols, last_x, *refs):
    count = len(refs) // 6
    tiles, halos, outs = refs[:count], refs[count : 2 * count], refs[2 * count :]
    for j in range(count):
        br, bc, scale, half = outs[4 * j : 4 * j + 4]
        blur_bands(rows, cols, last_x, held_taps(halos[j]), br, bc, scale)
        for i in range(2):
            half[i] = row_blur(rows, i, tiles[j], halos[j], br)


def row_blur(rows, i, tile, halo, br):
    field = [tile[i * rows : (i + 1) * rows, :], halo[16 * i : 16 * i + 128, :]]
    return dot(br[i], jnp.concatenate(field, 0)).astype(jnp.bfloat16)


def blur_bands(rows, cols, last_x, p, br_ref, bc_ref, scale_ref):
    out_rows, circle = br_ref.shape[1:]
    all_cols = bc_ref.shape[1]
    here_x = lax.axis_index("tx")
    odd = here_x % 2 > 0
    one = jnp.ones((16, 128), jnp.float32)
    keep_above = jnp.where(here_x > 0, one, 0.0).astype(jnp.bfloat16)
    keep_below = jnp.where(here_x < last_x, one, 0.0).astype(jnp.bfloat16)
    p = p / jnp.sum(p, axis=1, keepdims=True)
    taps = [p[:, t : t + 1] for t in range(2 * PR + 1)]
    kernels = (taps, [t * t for t in taps])
    row_base = (distance(circle, 1) + PR) & (circle - 1)
    col_base = distance(all_cols, 0) + PR
    col_base = jnp.where(col_base < 0, col_base + all_cols, col_base)
    lane = lax.broadcasted_iota(jnp.int32, (16, 128), 1)
    for i in range(2):
        rounded = sum(t.astype(jnp.bfloat16).astype(jnp.float32) for t in kernels[i])
        ratio = sum(kernels[i]) / rounded
        scale_ref[i] = jnp.broadcast_to(ratio * ratio, scale_ref.shape[1:])
        pieces = cut(select(row_base, kernels[i]))
        first_a = (RIM - 16) * i
        first_b = 2 * RIM + first_a

        def rim(n, lanes, coordinate):
            return jnp.where(
                (lane >= lanes) & (lane < lanes + RIM), turned(pieces, (n + lanes - coordinate) % circle), 0.0
            ).astype(jnp.bfloat16)

        for at in range(0, out_rows, 16):
            n = at if at < rows + REACH else at - out_rows
            left = turned(pieces, n % circle)
            right = jnp.zeros((16, 128), jnp.bfloat16)
            if n - PR < 0:
                right = jnp.where(odd, rim(n, first_a, -RIM), rim(n, first_b, -RIM))
            elif n + 16 + PR > rows:
                right = jnp.where(odd, rim(n, first_b, rows), rim(n, first_a, rows))
            if n < 0 or n >= rows:
                keep = keep_above if n < 0 else keep_below
                left, right = left * keep, right * keep
            br_ref[i, at : at + 16, :128] = left
            br_ref[i, at : at + 16, 128:] = right
        pieces = cut(select(col_base, kernels[i]))
        for n in range(0, all_cols, 16):
            bc_ref[i, n : n + 16, :] = turned(pieces, n)


def edge_kernel(*refs):
    out_ref = refs[-1]
    last = jnp.where(lax.axis_index("ty") == 0, jnp.ones((1, 128), jnp.float32), 0.0)
    first = (1.0 - last).astype(jnp.bfloat16)
    last = last.astype(jnp.bfloat16)
    at = 0
    for ref in refs[:-1]:
        rows, cols = ref.shape
        out_ref[at : at + rows, :] = ref[:, :128] * first + ref[:, cols - 128 :] * last
        at += rows


def dot(a, b):
    return jnp.dot(a, b, preferred_element_type=jnp.float32)


def widen(c, count):
    total = c.shape[0]
    return jnp.concatenate(
        [c] + [jnp.concatenate([c[total - 128 * j :], c[: total - 128 * j]], 0) for j in range(1, count)],
        1,
    )


def stack_kernel(slots, hyps, rows, cols, last_y, first, final, spots, *refs):
    count = len(slots)
    refs = list(refs)
    made, brs, bcs, scales = [[refs.pop(0) for _ in range(count)] for _ in range(4)]
    side_tiles, side_halos, rb, cb = [refs.pop(0) for _ in range(4)]
    acc = None if first else refs.pop(0)
    out = refs.pop(0)
    wide = cols + 128
    lane = lax.broadcasted_iota(jnp.int32, (1, 128), 1)
    here_y = lax.axis_index("ty")
    after = jnp.where((lane < 64) & (here_y < last_y), 1.0, 0.0)
    before = jnp.where((lane >= 64) & (here_y > 0), 1.0, 0.0)
    side = (after + before).astype(jnp.bfloat16)
    after = after.astype(jnp.bfloat16)
    before = before.astype(jnp.bfloat16)
    upper = rows + REACH
    unused = jnp.zeros((rb.shape[2] - rows - 2 * REACH, wide), jnp.float32)
    moved = []
    for j in range(count):
        pair = []
        tile_at, halo_at = spots[j]
        for i in range(2):
            at = i * rows
            rim = 16 * i
            right = [side_tiles[tile_at + at : tile_at + at + rows, :], side_halos[halo_at + rim : halo_at + rim + 128, :]]
            right = [
                x * side if x.shape[1] == 128 else x[:, :128] * after + x[:, cols - 128 :] * before
                for x in right
            ]
            right = jnp.concatenate(right, 0)
            half = jnp.concatenate([made[j][i], dot(brs[j][i], right).astype(jnp.bfloat16)], 1)
            image = dot(half, widen(bcs[j][i], wide // 128)) * scales[j][i, 0:1, :]
            image = jnp.concatenate([image[:upper], unused, image[upper:]], 0).astype(jnp.bfloat16)
            pair += [image[:, :cols], image[:, cols:] * side]
        moved.append(dot(rb[slots[j]], jnp.concatenate(pair, 1)).astype(jnp.bfloat16))
    copies = []
    for h in range(hyps):
        at = slice(h * rows, (h + 1) * rows)
        both = [jnp.concatenate([m[at, :wide], m[at, wide:]], 0) for m in moved]
        bands = [widen(cb[h, k], cols // 128) for k in slots]
        total = dot(jnp.concatenate(both, 1), jnp.concatenate(bands, 0))
        if not first:
            total = total + acc[h]
        if final:
            held, sems = refs
            held[h] = total[:rows] * lax.rsqrt(total[rows:])
            copies.append(pltpu.make_async_copy(held.at[h], out.at[h], sems.at[h]))
            copies[-1].start()
        else:
            out[h] = total
    for copy in copies:
        copy.wait()


VMEM = pl.BlockSpec(memory_space=pltpu.VMEM)
SMEM = pl.BlockSpec(memory_space=pltpu.SMEM)
PARAMS = pltpu.CompilerParams(vmem_limit_bytes=VMEM_LIMIT)


def call(kernel, specs, shapes, *args, scratch=(), flops=0, out=VMEM):
    single = not isinstance(shapes, (list, tuple))
    return pl.pallas_call(
        kernel,
        out_shape=shapes,
        in_specs=specs,
        out_specs=out if single else [out] * len(shapes),
        scratch_shapes=list(scratch),
        compiler_params=PARAMS,
        cost_estimate=pl.CostEstimate(flops=flops, bytes_accessed=0, transcendentals=0),
    )(*args)


def bf16(*shape):
    return jax.ShapeDtypeStruct(shape, jnp.bfloat16)


def side_swap(x):
    count = lax.axis_size("ty")
    if count == 2:
        return lax.ppermute(x, "ty", [(0, 1), (1, 0)])
    after = lax.ppermute(x[:, :128], "ty", [(i + 1, i) for i in range(count - 1)])
    before = lax.ppermute(x[:, x.shape[1] - 128 :], "ty", [(i, i + 1) for i in range(count - 1)])
    return jnp.concatenate([after, before], 1)


def shards(science, inv_variance, psf_taps, epoch_times, velocities):
    rows, cols = science.shape[1:]
    hyps = velocities.shape[0]
    epochs = lax.axis_size("ea")
    tx = lax.axis_size("tx")
    ty = lax.axis_size("ty")
    all_cols = cols + 128
    slots = min(GROUP, epochs)

    own = jnp.concatenate([science[0] * inv_variance[0], inv_variance[0]], 0).astype(jnp.bfloat16)
    tiles = [own] + [
        lax.ppermute(own, "ea", [(i, i ^ k) for i in range(epochs)]) for k in range(1, epochs)
    ]
    cut_from = own
    if epochs == slots:
        pass
    strip_a, strip_b = call(
        functools.partial(strip_kernel, rows),
        [VMEM],
        [bf16(2 * RIM, cols)] * 2,
        cut_from,
        flops=STRIP_FLOPS,
    )
    swap_b = [(i, i + 1) for i in range(1, tx - 1, 2)] + [(i + 1, i) for i in range(1, tx - 1, 2)]
    swap_a = [(i, i + 1) for i in range(0, tx - 1, 2)] + [(i + 1, i) for i in range(0, tx - 1, 2)]
    rim_b = lax.ppermute(strip_b, "tx", swap_b)
    rim_a = lax.ppermute(strip_a, "tx", swap_a)
    halo = call(rim_kernel, [VMEM] * 3, bf16(4 * RIM, cols), psf_taps, rim_a, rim_b, flops=STRIP_FLOPS)
    band_shapes = [
        bf16(2, rows + 2 * REACH, 2 * rows),
        bf16(2, all_cols, 128),
        jax.ShapeDtypeStruct((2, 8, all_cols), jnp.float32),
    ]

    def shift_bands(base):
        return call(
            functools.partial(shift_kernel, hyps, rows, all_cols),
            [SMEM] * 3,
            [bf16(slots, hyps * rows, 2 * rows), bf16(hyps, slots, all_cols, 128)],
            base,
            epoch_times,
            velocities,
            flops=SHIFT_FLOPS,
        )

    def blurred(tiles, halos):
        count = len(halos)
        made = call(
            functools.partial(blur_kernel, rows, cols, tx - 1),
            [VMEM] * (2 * count),
            [*band_shapes, bf16(2, rows + 2 * REACH, cols)] * count,
            *tiles,
            *halos,
            flops=BLUR_FLOPS,
        )
        return [made[j::4] for j in range(4)]

    def stack(slots, made, blurs, side_tiles, side_halos, shifts, total, final):
        args = [*made, *[x for kind in blurs for x in kind], side_tiles, side_halos, *shifts]
        if total is not None:
            args.append(total)
        shape = (hyps, rows, cols) if final else (hyps, 2 * rows, cols)
        shape = jax.ShapeDtypeStruct(shape, jnp.float32)
        spots = [(j * own.shape[0], j * halo.shape[0]) for j in range(len(slots))]
        return call(
            functools.partial(
                stack_kernel, slots, hyps, rows, cols, ty - 1, total is None, final, spots
            ),
            [VMEM] * len(args),
            shape,
            *args,
            flops=STACK_FLOPS,
            out=pl.BlockSpec(memory_space=pltpu.HBM) if final else VMEM,
            scratch=[pltpu.VMEM(shape.shape, jnp.float32), pltpu.SemaphoreType.DMA((hyps,))] if final else [],
        )

    def beside(arrays, narrow=False):
        if narrow and ty == 2:
            shape = bf16(sum(x.shape[0] for x in arrays), 128)
            return side_swap(call(edge_kernel, [VMEM] * len(arrays), shape, *arrays, flops=STRIP_FLOPS))
        return side_swap(jnp.concatenate(arrays, 0))

    if epochs == slots:
        shifts = shift_bands(jnp.zeros((1,), jnp.int32))
        *shifts, halo = lax.optimization_barrier((*shifts, halo))
        halos = [halo] + [
            lax.ppermute(halo, "ea", [(i, i ^ k) for i in range(epochs)]) for k in range(1, epochs)
        ]
        side = beside([own, halo])
        *blurs, made = blurred([own], [halo])
        total = stack([0], made, blurs, side[: own.shape[0]], side[own.shape[0] :], shifts, None, False)
        taken = [3, 1, 2]
        others = lax.optimization_barrier([tiles[k] for k in taken])
        others = [others[taken.index(k)] for k in range(1, epochs)]
        later = beside(others)
        taken = [1, 3, 2]
        total, later, *rest = lax.optimization_barrier((total, later, *[halos[k] for k in taken]))
        rims = [rest[taken.index(k)] for k in range(1, epochs)]
        *blurs, made = blurred(others, rims)
        return stack(list(range(1, epochs)), made, blurs, later, beside(rims, True), shifts, total, True)

    halos = [halo] + [
        lax.ppermute(halo, "ea", [(i, i ^ k) for i in range(epochs)]) for k in range(1, epochs)
    ]

    def step(total, xs):
        tiles, halos, base = xs
        tiles = [tiles[k] for k in range(slots)]
        halos = [halos[k] for k in range(slots)]
        *blurs, made = blurred(tiles, halos)
        sides = beside(tiles), beside(halos)
        return stack(list(range(slots)), made, blurs, *sides, shift_bands(base), total, False), None

    split = lambda x: x.reshape((epochs // slots, slots) + x.shape[1:])
    zeros = jnp.zeros((hyps, 2 * rows, cols), jnp.float32)
    bases = jnp.arange(0, epochs, slots, dtype=jnp.int32)[:, None]
    every = (split(jnp.stack(tiles)), split(jnp.stack(halos)), bases)
    total, _ = lax.scan(step, zeros, every)
    return total[:, :rows] / jnp.sqrt(total[:, rows:])


def solution(mesh):
    in_specs = (P("ea", "tx", "ty"), P("ea", "tx", "ty"), P("ea", None), P(), P("ea", None))
    out_specs = P("ea", "tx", "ty")
    return jax.shard_map(shards, mesh=mesh, in_specs=in_specs, out_specs=out_specs, check_vma=False)
```

```python
import functools

import jax
import jax.numpy as jnp
from jax import lax
from jax.experimental import pallas as pl
from jax.experimental.pallas import tpu as pltpu
from jax.sharding import PartitionSpec as P

REACH = 32
PR = 4
RIM = REACH + PR
GROUP = 4
VMEM_LIMIT = 24 * 1024 * 1024
STRIP_FLOPS = 4_000_000_000
SHIFT_FLOPS = 4_000_000_000
BLUR_FLOPS = 4_000_000_000
STACK_FLOPS = 2_000_000_000


def spline_taps(speed, time):
    moved = (speed * time) >> 3
    frac = (moved & 15).astype(jnp.float32) * (1.0 / 16.0)
    rest = 1.0 - frac
    frac2 = frac * frac
    frac3 = frac2 * frac
    sixth = 1.0 / 6.0
    weights = [
        rest * rest * rest * sixth,
        (3.0 * frac3 - 6.0 * frac2 + 4.0) * sixth,
        (-3.0 * frac3 + 3.0 * frac2 + 3.0 * frac + 1.0) * sixth,
        frac3 * sixth,
    ]
    return moved >> 4, weights


def strip_kernel(rows, own_ref, a_ref, b_ref):
    odd = lax.axis_index("tx") % 2 > 0
    heads, tails = [], []
    for i in range(2):
        x = own_ref[i * rows : (i + 1) * rows, :].astype(jnp.float32)
        heads.append(x[:RIM])
        tails.append(x[rows - RIM :])
    head = jnp.concatenate(heads, 0)
    tail = jnp.concatenate(tails, 0)
    a_ref[...] = jnp.where(odd, head, tail).astype(jnp.bfloat16)
    b_ref[...] = jnp.where(odd, tail, head).astype(jnp.bfloat16)


SPARE = ((0, RIM - 1), (RIM, 2 * RIM - 1), (3 * RIM - 1, 2 * RIM))


def rim_kernel(taps_ref, a_ref, b_ref, out_ref):
    odd = lax.axis_index("tx") % 2 > 0
    cols = out_ref.shape[1]
    taps = taps_ref[...]
    taps = jnp.concatenate([taps, jnp.zeros((1, cols - taps.shape[1]), jnp.float32)], 1)
    hi = taps.astype(jnp.bfloat16).astype(jnp.float32)
    mid = (taps - hi).astype(jnp.bfloat16).astype(jnp.float32)
    rims = jnp.concatenate([a_ref[...].astype(jnp.float32), b_ref[...].astype(jnp.float32)], 0)
    row = lax.broadcasted_iota(jnp.int32, rims.shape, 0)
    for (on_odd, on_even), part in zip(SPARE, (hi, mid, taps - hi - mid)):
        rims = jnp.where(row == jnp.where(odd, on_odd, on_even), part, rims)
    out_ref[...] = rims.astype(jnp.bfloat16)


def turned(pieces, by):
    count = len(pieces)
    whole, part = divmod(by, 128)
    near = pieces[-whole % count]
    if part == 0:
        return near
    far = pieces[(-whole - 1) % count]
    lane = lax.broadcasted_iota(jnp.int32, near.shape, 1)
    return jnp.where(lane >= part, pltpu.roll(near, part, 1), pltpu.roll(far, part, 1))


def cut(base):
    return [base[:, j : j + 128] for j in range(0, base.shape[1], 128)]


def select(d, weights):
    acc = jnp.zeros(d.shape, jnp.float32)
    for a, w in enumerate(weights):
        acc = jnp.where(d == a, w, acc)
    return acc.astype(jnp.bfloat16)


def distance(count, source_axis):
    d = lax.broadcasted_iota(jnp.int32, (16, count), source_axis) - lax.broadcasted_iota(
        jnp.int32, (16, count), 1 - source_axis
    )
    return d


def shift_kernel(hyps, rows, all_cols, base_ref, times_ref, speed_ref, rb_ref, cb_ref):
    circle = rb_ref.shape[2]
    row_base = distance(circle, 1)
    col_base = distance(all_cols, 0)

    def one(e, carry):
        time = times_ref[lax.axis_index("ea") ^ (base_ref[0] + e)]
        for h in range(hyps):
            whole, weights = spline_taps(speed_ref[h, 0], time)
            pieces = cut(select((row_base - (whole - 1)) & (circle - 1), weights))
            turns = [pieces[-j:] + pieces[:-j] for j in range(len(pieces), 0, -1)]
            for n in range(0, rows, 16):
                for j, turn in enumerate(turns):
                    rb_ref[e, h * rows + n : h * rows + n + 16, 128 * j : 128 * (j + 1)] = turned(turn, n)
            whole, weights = spline_taps(speed_ref[h, 1], time)
            d = col_base - (whole - 1)
            pieces = cut(select(jnp.where(d < 0, d + all_cols, d), weights))
            for n in range(0, all_cols, 16):
                cb_ref[h, e, n : n + 16, :] = turned(pieces, n)
        return carry

    lax.fori_loop(0, rb_ref.shape[0], one, 0)


def held_taps(halo_ref):
    odd = lax.axis_index("tx") % 2 > 0

    def held(row):
        block = halo_ref[row // 16 * 16 : row // 16 * 16 + 16, :].astype(jnp.float32)
        return block[row % 16 : row % 16 + 1]

    return sum(jnp.where(odd, held(on_odd), held(on_even)) for on_odd, on_even in SPARE)


def blur_kernel(rows, cols, last_x, *refs):
    count = len(refs) // 6
    tiles, halos, outs = refs[:count], refs[count : 2 * count], refs[2 * count :]
    for j in range(count):
        br, bc, scale, half = outs[4 * j : 4 * j + 4]
        blur_bands(rows, cols, last_x, held_taps(halos[j]), br, bc, scale)
        for i in range(2):
            half[i] = row_blur(rows, i, tiles[j], halos[j], br)


def row_blur(rows, i, tile, halo, br):
    field = [tile[i * rows : (i + 1) * rows, :], halo[16 * i : 16 * i + 128, :]]
    return dot(br[i], jnp.concatenate(field, 0)).astype(jnp.bfloat16)


def blur_bands(rows, cols, last_x, p, br_ref, bc_ref, scale_ref):
    out_rows, circle = br_ref.shape[1:]
    all_cols = bc_ref.shape[1]
    here_x = lax.axis_index("tx")
    odd = here_x % 2 > 0
    one = jnp.ones((16, 128), jnp.float32)
    keep_above = jnp.where(here_x > 0, one, 0.0).astype(jnp.bfloat16)
    keep_below = jnp.where(here_x < last_x, one, 0.0).astype(jnp.bfloat16)
    p = p / jnp.sum(p, axis=1, keepdims=True)
    taps = [p[:, t : t + 1] for t in range(2 * PR + 1)]
    kernels = (taps, [t * t for t in taps])
    row_base = (distance(circle, 1) + PR) & (circle - 1)
    col_base = distance(all_cols, 0) + PR
    col_base = jnp.where(col_base < 0, col_base + all_cols, col_base)
    lane = lax.broadcasted_iota(jnp.int32, (16, 128), 1)
    for i in range(2):
        rounded = sum(t.astype(jnp.bfloat16).astype(jnp.float32) for t in kernels[i])
        ratio = sum(kernels[i]) / rounded
        scale_ref[i] = jnp.broadcast_to(ratio * ratio, scale_ref.shape[1:])
        pieces = cut(select(row_base, kernels[i]))
        first_a = (RIM - 16) * i
        first_b = 2 * RIM + first_a

        def rim(n, lanes, coordinate):
            return jnp.where(
                (lane >= lanes) & (lane < lanes + RIM), turned(pieces, (n + lanes - coordinate) % circle), 0.0
            ).astype(jnp.bfloat16)

        for at in range(0, out_rows, 16):
            n = at if at < rows + REACH else at - out_rows
            left = turned(pieces, n % circle)
            right = jnp.zeros((16, 128), jnp.bfloat16)
            if n - PR < 0:
                right = jnp.where(odd, rim(n, first_a, -RIM), rim(n, first_b, -RIM))
            elif n + 16 + PR > rows:
                right = jnp.where(odd, rim(n, first_b, rows), rim(n, first_a, rows))
            if n < 0 or n >= rows:
                keep = keep_above if n < 0 else keep_below
                left, right = left * keep, right * keep
            br_ref[i, at : at + 16, :128] = left
            br_ref[i, at : at + 16, 128:] = right
        pieces = cut(select(col_base, kernels[i]))
        for n in range(0, all_cols, 16):
            bc_ref[i, n : n + 16, :] = turned(pieces, n)


def edge_kernel(*refs):
    out_ref = refs[-1]
    last = jnp.where(lax.axis_index("ty") == 0, jnp.ones((1, 128), jnp.float32), 0.0)
    first = (1.0 - last).astype(jnp.bfloat16)
    last = last.astype(jnp.bfloat16)
    at = 0
    for ref in refs[:-1]:
        rows, cols = ref.shape
        out_ref[at : at + rows, :] = ref[:, :128] * first + ref[:, cols - 128 :] * last
        at += rows


def dot(a, b):
    return jnp.dot(a, b, preferred_element_type=jnp.float32)


def widen(c, count):
    total = c.shape[0]
    return jnp.concatenate(
        [c] + [jnp.concatenate([c[total - 128 * j :], c[: total - 128 * j]], 0) for j in range(1, count)],
        1,
    )


def stack_kernel(slots, hyps, rows, cols, last_y, first, final, spots, *refs):
    count = len(slots)
    refs = list(refs)
    made, brs, bcs, scales = [[refs.pop(0) for _ in range(count)] for _ in range(4)]
    side_tiles, side_halos, rb, cb = [refs.pop(0) for _ in range(4)]
    acc = None if first else refs.pop(0)
    out = refs.pop(0)
    wide = cols + 128
    lane = lax.broadcasted_iota(jnp.int32, (1, 128), 1)
    here_y = lax.axis_index("ty")
    after = jnp.where((lane < 64) & (here_y < last_y), 1.0, 0.0)
    before = jnp.where((lane >= 64) & (here_y > 0), 1.0, 0.0)
    side = (after + before).astype(jnp.bfloat16)
    after = after.astype(jnp.bfloat16)
    before = before.astype(jnp.bfloat16)
    upper = rows + REACH
    unused = jnp.zeros((rb.shape[2] - rows - 2 * REACH, wide), jnp.float32)
    moved = []
    for j in range(count):
        pair = []
        tile_at, halo_at = spots[j]
        for i in range(2):
            at = i * rows
            rim = 16 * i
            right = [side_tiles[tile_at + at : tile_at + at + rows, :], side_halos[halo_at + rim : halo_at + rim + 128, :]]
            right = [
                x * side if x.shape[1] == 128 else x[:, :128] * after + x[:, cols - 128 :] * before
                for x in right
            ]
            right = jnp.concatenate(right, 0)
            half = jnp.concatenate([made[j][i], dot(brs[j][i], right).astype(jnp.bfloat16)], 1)
            image = dot(half, widen(bcs[j][i], wide // 128)) * scales[j][i, 0:1, :]
            image = jnp.concatenate([image[:upper], unused, image[upper:]], 0).astype(jnp.bfloat16)
            pair += [image[:, :cols], image[:, cols:] * side]
        moved.append(dot(rb[slots[j]], jnp.concatenate(pair, 1)).astype(jnp.bfloat16))
    copies = []
    for h in range(hyps):
        at = slice(h * rows, (h + 1) * rows)
        both = [jnp.concatenate([m[at, :wide], m[at, wide:]], 0) for m in moved]
        bands = [widen(cb[h, k], cols // 128) for k in slots]
        total = dot(jnp.concatenate(both, 1), jnp.concatenate(bands, 0))
        if not first:
            total = total + acc[h]
        if final:
            held, sems = refs
            held[h] = total[:rows] * lax.rsqrt(total[rows:])
            copies.append(pltpu.make_async_copy(held.at[h], out.at[h], sems.at[h]))
            copies[-1].start()
        else:
            out[h] = total
    for copy in copies:
        copy.wait()


VMEM = pl.BlockSpec(memory_space=pltpu.VMEM)
SMEM = pl.BlockSpec(memory_space=pltpu.SMEM)
PARAMS = pltpu.CompilerParams(vmem_limit_bytes=VMEM_LIMIT)


def call(kernel, specs, shapes, *args, scratch=(), flops=0, out=VMEM):
    single = not isinstance(shapes, (list, tuple))
    return pl.pallas_call(
        kernel,
        out_shape=shapes,
        in_specs=specs,
        out_specs=out if single else [out] * len(shapes),
        scratch_shapes=list(scratch),
        compiler_params=PARAMS,
        cost_estimate=pl.CostEstimate(flops=flops, bytes_accessed=0, transcendentals=0),
    )(*args)


def bf16(*shape):
    return jax.ShapeDtypeStruct(shape, jnp.bfloat16)


def side_swap(x):
    count = lax.axis_size("ty")
    if count == 2:
        return lax.ppermute(x, "ty", [(0, 1), (1, 0)])
    after = lax.ppermute(x[:, :128], "ty", [(i + 1, i) for i in range(count - 1)])
    before = lax.ppermute(x[:, x.shape[1] - 128 :], "ty", [(i, i + 1) for i in range(count - 1)])
    return jnp.concatenate([after, before], 1)


def shards(science, inv_variance, psf_taps, epoch_times, velocities):
    rows, cols = science.shape[1:]
    hyps = velocities.shape[0]
    epochs = lax.axis_size("ea")
    tx = lax.axis_size("tx")
    ty = lax.axis_size("ty")
    all_cols = cols + 128
    slots = min(GROUP, epochs)

    own = jnp.concatenate([science[0] * inv_variance[0], inv_variance[0]], 0).astype(jnp.bfloat16)
    tiles = [own] + [
        lax.ppermute(own, "ea", [(i, i ^ k) for i in range(epochs)]) for k in range(1, epochs)
    ]
    cut_from = own
    if epochs == slots:
        pass
    strip_a, strip_b = call(
        functools.partial(strip_kernel, rows),
        [VMEM],
        [bf16(2 * RIM, cols)] * 2,
        cut_from,
        flops=STRIP_FLOPS,
    )
    swap_b = [(i, i + 1) for i in range(1, tx - 1, 2)] + [(i + 1, i) for i in range(1, tx - 1, 2)]
    swap_a = [(i, i + 1) for i in range(0, tx - 1, 2)] + [(i + 1, i) for i in range(0, tx - 1, 2)]
    rim_b = lax.ppermute(strip_b, "tx", swap_b)
    rim_a = lax.ppermute(strip_a, "tx", swap_a)
    halo = call(rim_kernel, [VMEM] * 3, bf16(4 * RIM, cols), psf_taps, rim_a, rim_b, flops=STRIP_FLOPS)
    band_shapes = [
        bf16(2, rows + 2 * REACH, 2 * rows),
        bf16(2, all_cols, 128),
        jax.ShapeDtypeStruct((2, 8, all_cols), jnp.float32),
    ]

    def shift_bands(base):
        return call(
            functools.partial(shift_kernel, hyps, rows, all_cols),
            [SMEM] * 3,
            [bf16(slots, hyps * rows, 2 * rows), bf16(hyps, slots, all_cols, 128)],
            base,
            epoch_times,
            velocities,
            flops=SHIFT_FLOPS,
        )

    def blurred(tiles, halos):
        count = len(halos)
        made = call(
            functools.partial(blur_kernel, rows, cols, tx - 1),
            [VMEM] * (2 * count),
            [*band_shapes, bf16(2, rows + 2 * REACH, cols)] * count,
            *tiles,
            *halos,
            flops=BLUR_FLOPS,
        )
        return [made[j::4] for j in range(4)]

    def stack(slots, made, blurs, side_tiles, side_halos, shifts, total, final):
        args = [*made, *[x for kind in blurs for x in kind], side_tiles, side_halos, *shifts]
        if total is not None:
            args.append(total)
        shape = (hyps, rows, cols) if final else (hyps, 2 * rows, cols)
        shape = jax.ShapeDtypeStruct(shape, jnp.float32)
        spots = [(j * own.shape[0], j * halo.shape[0]) for j in range(len(slots))]
        return call(
            functools.partial(
                stack_kernel, slots, hyps, rows, cols, ty - 1, total is None, final, spots
            ),
            [VMEM] * len(args),
            shape,
            *args,
            flops=STACK_FLOPS,
            out=pl.BlockSpec(memory_space=pltpu.HBM) if final else VMEM,
            scratch=[pltpu.VMEM(shape.shape, jnp.float32), pltpu.SemaphoreType.DMA((hyps,))] if final else [],
        )

    def beside(arrays, narrow=False):
        if narrow and ty == 2:
            shape = bf16(sum(x.shape[0] for x in arrays), 128)
            return side_swap(call(edge_kernel, [VMEM] * len(arrays), shape, *arrays, flops=STRIP_FLOPS))
        return side_swap(jnp.concatenate(arrays, 0))

    if epochs == slots:
        shifts = shift_bands(jnp.zeros((1,), jnp.int32))
        *shifts, halo = lax.optimization_barrier((*shifts, halo))
        halos = [halo] + [
            lax.ppermute(halo, "ea", [(i, i ^ k) for i in range(epochs)]) for k in range(1, epochs)
        ]
        side = beside([own, halo], True)
        *blurs, made = blurred([own], [halo])
        total = stack([0], made, blurs, side[: own.shape[0]], side[own.shape[0] :], shifts, None, False)
        taken = [3, 1, 2]
        others = lax.optimization_barrier([tiles[k] for k in taken])
        others = [others[taken.index(k)] for k in range(1, epochs)]
        later = beside(others)
        taken = [1, 3, 2]
        total, later, *rest = lax.optimization_barrier((total, later, *[halos[k] for k in taken]))
        rims = [rest[taken.index(k)] for k in range(1, epochs)]
        *blurs, made = blurred(others, rims)
        return stack(list(range(1, epochs)), made, blurs, later, beside(rims, True), shifts, total, True)

    halos = [halo] + [
        lax.ppermute(halo, "ea", [(i, i ^ k) for i in range(epochs)]) for k in range(1, epochs)
    ]

    def step(total, xs):
        tiles, halos, base = xs
        tiles = [tiles[k] for k in range(slots)]
        halos = [halos[k] for k in range(slots)]
        *blurs, made = blurred(tiles, halos)
        sides = beside(tiles), beside(halos)
        return stack(list(range(slots)), made, blurs, *sides, shift_bands(base), total, False), None

    split = lambda x: x.reshape((epochs // slots, slots) + x.shape[1:])
    zeros = jnp.zeros((hyps, 2 * rows, cols), jnp.float32)
    bases = jnp.arange(0, epochs, slots, dtype=jnp.int32)[:, None]
    every = (split(jnp.stack(tiles)), split(jnp.stack(halos)), bases)
    total, _ = lax.scan(step, zeros, every)
    return total[:, :rows] / jnp.sqrt(total[:, rows:])


def solution(mesh):
    in_specs = (P("ea", "tx", "ty"), P("ea", "tx", "ty"), P("ea", None), P(), P("ea", None))
    out_specs = P("ea", "tx", "ty")
    return jax.shard_map(shards, mesh=mesh, in_specs=in_specs, out_specs=out_specs, check_vma=False)
```
